256 devices in a mesh: tm: 32 (over x_hi, z, core), space: 8 (over y, x_lo).
Axes of the slice: x: 4 (x_hi: 2, x_lo: 2; x = x_hi * 2 + x_lo), y: 4, z: 8, core: 2. Of those that a mesh axis runs over, the one named last changes fastest.
Arguments:
- queries: bfloat16 [32768, 1536], P(('tm', 'space')), may hold values from -24 to 24
- keys: bfloat16 [32768, 1536], P(('tm', 'space')), may hold values from -24 to 24
- values: bfloat16 [32768, 1536], P(('tm', 'space')), may hold values from -8 to 8
- tile_mask: int32 [32, 32], replicated, may hold values from 0 to 1, as said below
- inner_x: bfloat16 [32768, 1536], P(('tm', 'space')), may hold values from -140 to 140
- bc_proj: bfloat16 [32768, 128], P(('tm', 'space')), may hold values from -4 to 4
- log_decay: bfloat16 [24, 32768], P(None, ('tm', 'space')), may hold values from -1 to 0
- col_order: int32 [32], replicated, may hold values from 0 to 31, each once
- norm_gain: float32 [1536], replicated, may hold values from 0.1 to 1.9
Outputs:
- mixed: bfloat16 [32768, 1536], P(('tm', 'space'))
The draws below stay inside these ranges and needn't reach their ends.
Inputs may be any that keep to these rules, and one draw needn't show every extreme that they name: `tile_mask`: 1 on the diagonal and for frames exactly 8 before or after around the loop; 0 for frames more than 8 away around the loop.
All inputs are finite; a program needn't handle non-finite values.
Results may differ from the reference program's by a relative error of at most 0.017.
Values may be sent and summed in bfloat16 or wider, within the bound.
No kernel may reach another device: no remote copies, remote signals or barrier semaphores. Data moves between devices by JAX's collectives and lax.ppermute only.
A program may use at most 384 MiB of HBM per device.

```python
import math
import jax
import jax.numpy as jnp
from jax import lax

HEADS = 12
HEAD_DIM = 128
SCAN_HEADS = 24
SCAN_DIM = 64
STATE_DIM = 64
ROWS_DEV = 4
COLS = 32
TOK_DEV = 128
FRAMES = 32
REACH = 8
HEIGHT = 32
VIDEO_ELEMENTS = 32768
N_TM = 32
N_SPACE = 8


def draw_queries(key, part):
    key = jax.random.fold_in(key, 1)
    drawn_rows = jnp.clip(jax.random.normal(key, (VIDEO_ELEMENTS, HEADS * HEAD_DIM), jnp.float32), -4.5, 4.5)
    return (1.41 * drawn_rows).astype(jnp.bfloat16)


def draw_keys(key, part):
    key = jax.random.fold_in(key, 2)
    drawn_rows = jnp.clip(jax.random.normal(key, (VIDEO_ELEMENTS, HEADS * HEAD_DIM), jnp.float32), -4.5, 4.5)
    return (1.41 * drawn_rows).astype(jnp.bfloat16)


def draw_tile_mask(key, part):
    key = jax.random.fold_in(key, 5)
    row_ids = jnp.arange(FRAMES)[:, None]
    col_ids = jnp.arange(FRAMES)[None, :]
    distance = jnp.minimum((col_ids - row_ids) % FRAMES, (row_ids - col_ids) % FRAMES)
    coin_flip = jax.random.randint(key, (FRAMES, FRAMES), 0, 2)
    inside = jnp.where(distance < REACH, coin_flip, 0)
    return jnp.where((distance == 0) | (distance == REACH), 1, inside).astype(jnp.int32)


def draw_inner_x(key, part):
    key = jax.random.fold_in(key, 7)
    sampler_seeds = jax.random.split(key, 3)
    width = SCAN_HEADS * SCAN_DIM
    core_values = jnp.clip(jax.random.normal(sampler_seeds[0], (VIDEO_ELEMENTS, width), jnp.float32), -4.0, 4.0)
    row_scale = 10.0 ** jax.random.uniform(sampler_seeds[1], (VIDEO_ELEMENTS, 1), jnp.float32)
    col_scale = 10.0 ** jax.random.uniform(sampler_seeds[2], (1, width), jnp.float32)
    return (0.25 * core_values * row_scale * col_scale).astype(jnp.bfloat16)


def draw_log_decay(key, part):
    key = jax.random.fold_in(key, 9)
    sampler_seeds = jax.random.split(key, 8)
    slow_share = 0.5
    middle_share = 0.3
    roughness = 0.5
    head_draw = jax.random.uniform(sampler_seeds[0], (SCAN_HEADS, 1), jnp.float32)
    slow_rate_flag = (head_draw < slow_share).astype(jnp.float32)
    medium_rate_flag = ((head_draw >= slow_share) & (head_draw < slow_share + middle_share)).astype(jnp.float32)
    rapid_indicator = 1.0 - slow_rate_flag - medium_rate_flag
    slow_rate = 0.3 / VIDEO_ELEMENTS * 10.0 ** jax.random.uniform(sampler_seeds[1], (SCAN_HEADS, 1), jnp.float32, -0.3, 0.0)
    middle_low = math.log10(0.4 / (HEIGHT * COLS))
    middle_high = math.log10(0.5 / TOK_DEV)
    middle_rate = 10.0 ** jax.random.uniform(sampler_seeds[7], (SCAN_HEADS, 1), jnp.float32, middle_low, middle_high)
    fast_rate = 10.0 ** jax.random.uniform(sampler_seeds[2], (SCAN_HEADS, 1), jnp.float32, math.log10(1.0 / 50.0), math.log10(1.0 / 30.0))
    decay_speed = slow_rate_flag * slow_rate + medium_rate_flag * middle_rate + rapid_indicator * fast_rate
    device_share_factor = 2.0 ** jax.random.uniform(sampler_seeds[3], (SCAN_HEADS, VIDEO_ELEMENTS // TOK_DEV), jnp.float32, -1.0, 1.0)
    device_share_factor = jnp.repeat(device_share_factor, TOK_DEV, axis=1)
    entry_multiplier = jax.random.uniform(sampler_seeds[4], (SCAN_HEADS, VIDEO_ELEMENTS), jnp.float32, 1.0 - roughness, 1.0 + roughness)
    spike_positions_list = jax.random.randint(sampler_seeds[5], (2,), 0, VIDEO_ELEMENTS)
    spike_reductions = jnp.log(jax.random.uniform(sampler_seeds[6], (2,), jnp.float32, 0.5, 0.8))
    affected_spots = (jnp.arange(VIDEO_ELEMENTS)[None, :] == spike_positions_list[:, None]).astype(jnp.float32)
    steep_decay = jnp.sum(affected_spots * spike_reductions[:, None], axis=0)
    spike_heads = slow_rate_flag + medium_rate_flag
    return (-(decay_speed * device_share_factor * entry_multiplier) + spike_heads * steep_decay[None, :]).astype(jnp.bfloat16)


def steps_of(key, extent, shards, smallest, top_value):
    gain, own = 1.0, jax.random.fold_in(key, 6)
    for dim, shards_of in shards:
        steps = jnp.exp(jax.random.uniform(jax.random.fold_in(own, dim), (shards_of,), jnp.float32, smallest / len(shards), top_value / len(shards)))
        gain = gain * jnp.repeat(steps, extent[dim] // shards_of).reshape([-1 if axis == dim else 1 for axis in range(len(extent))])
    return gain


def gaussian(rng, dims, scale, most, shards=(), kind=jnp.bfloat16):
    result = jax.random.normal(rng, dims, jnp.float32) * scale
    if len(shards) > 0:
        result = steps_of(rng, dims, shards, -0.22, 0.18) * result
    return jnp.clip(result, min=-most, max=most).astype(kind)


def setup_inputs(seed: int = 0) -> dict:
    key_list = jax.random.split(jax.random.key(seed), 10)
    queries = draw_queries(jax.random.fold_in(key_list[9], 71), 0)
    keys = draw_keys(jax.random.fold_in(key_list[9], 71), 0)
    values = gaussian(key_list[2], (VIDEO_ELEMENTS, HEADS * HEAD_DIM), 2.0, 8.0, ((0, 256),))
    tile_mask = draw_tile_mask(jax.random.fold_in(key_list[9], 71), 0)
    inner_x = draw_inner_x(jax.random.fold_in(key_list[9], 71), 0)
    bc_proj = gaussian(key_list[5], (VIDEO_ELEMENTS, 2 * STATE_DIM), 0.3, 4.0, ((0, 256),))
    log_decay = draw_log_decay(jax.random.fold_in(key_list[9], 71), 0)
    col_order = jax.random.permutation(key_list[7], COLS).astype(jnp.int32)
    norm_gain = jnp.clip(1.0 + 0.18 * jax.random.normal(key_list[8], (SCAN_HEADS * SCAN_DIM,), jnp.float32), 0.1, 1.9)
    return dict(queries=queries, keys=keys, values=values, tile_mask=tile_mask, inner_x=inner_x, bc_proj=bc_proj, log_decay=log_decay, col_order=col_order, norm_gain=norm_gain)


EPS = 1e-05
FLOOR = -1e+30

def block_terms(x_block, b_proj, log_rates):
    cumlog = jnp.cumsum(log_rates, axis=1)
    log_total = cumlog[:, -1]
    weights = (jnp.exp(log_total[:, None] - cumlog)[:, :, None] * b_proj.astype(jnp.float32)[None]).astype(jnp.bfloat16)
    local_state = jnp.einsum('hjn,jhp->hnp', weights.astype(jnp.float32), x_block.astype(jnp.float32))
    return (cumlog, log_total, local_state)

def block_output(x_block, b_proj, c_proj, cumlog, carried):
    length = x_block.shape[0]
    pair_scores = jnp.dot(c_proj, b_proj.T, preferred_element_type=jnp.float32)
    lower_mask = jnp.arange(length, dtype=jnp.int32)[:, None] >= jnp.arange(length, dtype=jnp.int32)[None, :]
    log_gap = jnp.where(lower_mask[None], cumlog[:, :, None] - cumlog[:, None, :], FLOOR)
    mixer = (pair_scores[None] * jnp.exp(log_gap)).astype(jnp.bfloat16)
    inside = jnp.einsum('hij,jhp->ihp', mixer.astype(jnp.float32), x_block.astype(jnp.float32))
    carried_out = jnp.einsum('in,hnp->ihp', c_proj.astype(jnp.float32), carried, precision=lax.Precision.HIGHEST)
    return inside + jnp.exp(cumlog).T[:, :, None] * carried_out

def run_scan(inner_rows, bc_rows, log_rows):
    blocks = inner_rows.shape[0] // TOK_DEV
    x_blocks = inner_rows.reshape(blocks, TOK_DEV, SCAN_HEADS, SCAN_DIM)
    bc_blocks = bc_rows.reshape(blocks, TOK_DEV, 2 * STATE_DIM)
    log_blocks = log_rows.astype(jnp.float32).reshape(blocks, TOK_DEV, SCAN_HEADS).transpose(0, 2, 1)

    def advance(carried, block_items):
        x_block, bc_block, log_block = block_items
        b_proj = bc_block[:, :STATE_DIM]
        c_proj = bc_block[:, STATE_DIM:]
        cumlog, log_total, local_state = block_terms(x_block, b_proj, log_block)
        output = block_output(x_block, b_proj, c_proj, cumlog, carried)
        return (jnp.exp(log_total)[:, None, None] * carried + local_state, output)
    start_state = jnp.zeros((SCAN_HEADS, STATE_DIM, SCAN_DIM), jnp.float32)
    _, outputs = lax.scan(advance, start_state, (x_blocks, bc_blocks, log_blocks))
    return outputs.reshape(-1, SCAN_HEADS, SCAN_DIM)

def reference(queries, keys, values, tile_mask, inner_x, bc_proj, log_decay, col_order, norm_gain):
    score_scale = HEAD_DIM ** (-0.5)
    feat_width = HEADS * HEAD_DIM
    query_grid = queries.reshape(N_TM, N_SPACE, TOK_DEV, HEADS, HEAD_DIM)
    key_grid = keys.reshape(N_TM, N_SPACE, TOK_DEV, HEADS, HEAD_DIM)
    value_grid = values.reshape(N_TM, N_SPACE, TOK_DEV, HEADS, HEAD_DIM)
    offsets = jnp.arange(-REACH, REACH + 1, dtype=jnp.int32)

    def attend(block_index):
        frame_idx = block_index // N_SPACE
        space_idx = block_index % N_SPACE
        near_frames = ((frame_idx + offsets) % N_TM).astype(jnp.int32)
        query_block = query_grid[frame_idx, space_idx]
        key_block = key_grid[near_frames, space_idx].reshape(-1, HEADS, HEAD_DIM)
        value_block = value_grid[near_frames, space_idx].reshape(-1, HEADS, HEAD_DIM)
        allowed = jnp.repeat(tile_mask[frame_idx, near_frames] > 0, TOK_DEV)
        scores = jnp.einsum('qhd,khd->hqk', query_block.astype(jnp.float32), key_block.astype(jnp.float32)) * score_scale
        scores = jnp.where(allowed[None, None, :], scores, FLOOR)
        row_max = lax.optimization_barrier(jnp.max(scores, axis=2, keepdims=True))
        probs = jnp.where(allowed[None, None, :], jnp.exp(scores - row_max), 0.0)
        denom = lax.optimization_barrier(jnp.sum(probs, axis=2))
        output = jnp.einsum('hqk,khd->qhd', probs.astype(jnp.bfloat16).astype(jnp.float32), value_block.astype(jnp.float32))
        return (output / denom.T[:, :, None]).reshape(TOK_DEV, feat_width)
    attention = lax.map(attend, jnp.arange(N_TM * N_SPACE, dtype=jnp.int32)).reshape(-1, feat_width)
    log_rows = log_decay.T
    row_out = run_scan(inner_x.reshape(-1, SCAN_HEADS, SCAN_DIM), bc_proj, log_rows)
    height = ROWS_DEV * N_SPACE

    def to_columns(grid):
        grid = grid.reshape(N_TM, height, COLS, grid.shape[-1])[:, :, col_order]
        return grid.transpose(0, 2, 1, 3).reshape(-1, grid.shape[-1])
    col_scan = run_scan(to_columns(inner_x).reshape(-1, SCAN_HEADS, SCAN_DIM), to_columns(bc_proj), to_columns(log_rows))
    col_scan = col_scan.astype(jnp.bfloat16).reshape(N_TM, COLS, height, SCAN_HEADS * SCAN_DIM).transpose(0, 2, 1, 3)
    col_rows = jnp.zeros_like(col_scan).at[:, :, col_order].set(col_scan)
    col_rows = col_rows.reshape(-1, SCAN_HEADS, SCAN_DIM).astype(jnp.float32)
    combined = row_out + col_rows
    meansq = lax.optimization_barrier(jnp.mean(combined * combined, axis=2, keepdims=True))
    normed = combined * lax.rsqrt(meansq + EPS) * norm_gain.reshape(SCAN_HEADS, SCAN_DIM)
    return (attention + normed.reshape(-1, SCAN_HEADS * SCAN_DIM)).astype(jnp.bfloat16)
```

```python
import functools
import math

import jax
import jax.numpy as jnp
from jax import lax
from jax.experimental import pallas as pl
from jax.experimental.pallas import tpu as pltpu
from jax.sharding import PartitionSpec as P

HEADS = 12
HEAD_DIM = 128
SCAN_HEADS = 24
SCAN_DIM = 64
STATE_DIM = 64
COLS = 32
TOKENS = 128
N_TM = 32
N_SPACE = 8
GROUP = HEADS // 4 * HEAD_DIM
WIN = 256
ROWS = STATE_DIM + 8

EPS = 1e-05
FLOOR = -1e30
LOG2_SCALE = HEAD_DIM ** (-0.5) * math.log2(math.e)
BF16 = jnp.bfloat16
F32 = jnp.float32

VMEM = pl.BlockSpec(memory_space=pltpu.VMEM)
SMEM = pl.BlockSpec(memory_space=pltpu.SMEM)


def call(body, out_shape, n_smem, n_vmem, scratch=(), flops=0, moved=0, aliases=None):
    return pl.pallas_call(
        body,
        out_shape=out_shape,
        in_specs=[SMEM] * n_smem + [VMEM] * n_vmem,
        out_specs=jax.tree.map(lambda _: VMEM, out_shape),
        scratch_shapes=list(scratch),
        input_output_aliases=aliases or {},
        compiler_params=pltpu.CompilerParams(vmem_limit_bytes=24 * 2**20),
        cost_estimate=pl.CostEstimate(flops=flops, bytes_accessed=moved, transcendentals=0),
    )


def dot(a, b, contract=(1, 0)):
    return lax.dot_general(
        a, b, (((contract[0],), (contract[1],)), ((), ())), preferred_element_type=F32
    )


def iota(shape, axis):
    return lax.broadcasted_iota(jnp.int32, shape, axis)


def head_groups(ids, q_ref, k_ref, v_ref, *outs):
    group = ids[0]
    for i, out in enumerate(outs):
        cols = pl.ds(pl.multiple_of((group ^ i) * GROUP, 128), GROUP)
        out[0] = q_ref[:, cols]
        out[1] = k_ref[:, cols]
        out[2] = v_ref[:, cols]


def absorb(ids, mask_ref, q_ref, kv_ref, m_ref, l_ref, acc_ref, source, delta, query, first):
    group, place = ids[0], ids[1]
    half, core = group // 2, group % 2
    there = place + delta
    wrapped = jnp.where((there < 0) | (there > 7), 1, 0)
    there = there & 7
    u = source ^ wrapped if query is None else query
    if first:
        u = query
    lanes = iota((1, 2 * TOKENS), 1)

    def bias(j):
        frame_k = 16 * (half ^ source) + 2 * there + (core ^ j)

        def one(a):
            frame_q = 16 * (half ^ u) + 2 * place + (core ^ a)
            return jnp.where(mask_ref[frame_q, frame_k] > 0, 0.0, FLOOR).astype(F32)

        return jnp.where(lanes < TOKENS, one(0), one(1))

    bias0, bias1 = bias(0), bias(1)
    for h in range(GROUP // HEAD_DIM):
        cols = slice(h * HEAD_DIM, (h + 1) * HEAD_DIM)
        q = q_ref[u, :, :, cols].reshape(2 * TOKENS, HEAD_DIM)
        k = kv_ref[:, 0, :, cols].reshape(2 * TOKENS, HEAD_DIM)
        v = kv_ref[:, 1, :, cols].reshape(2 * TOKENS, HEAD_DIM)
        scores = dot(k, q, (1, 1))
        s0, s1 = scores[:TOKENS], scores[TOKENS:]
        top = jnp.maximum(
            jnp.max(s0, axis=0, keepdims=True) * LOG2_SCALE + bias0,
            jnp.max(s1, axis=0, keepdims=True) * LOG2_SCALE + bias1,
        )
        if not first:
            old = m_ref[u, h : h + 1, :]
            top = jnp.maximum(top, old)
        p0 = jnp.exp2(s0 * LOG2_SCALE + (bias0 - top))
        p1 = jnp.exp2(s1 * LOG2_SCALE + (bias1 - top))
        total = jnp.sum(p0 + p1, axis=0, keepdims=True)
        probs = jnp.concatenate([p0.astype(BF16), p1.astype(BF16)], axis=0)
        update = dot(v, probs, (0, 0))
        if first:
            l_ref[u, h : h + 1, :] = total
            acc_ref[u, h] = update
        else:
            factor = jnp.exp2(old - top)
            l_ref[u, h : h + 1, :] = l_ref[u, h : h + 1, :] * factor + total
            acc_ref[u, h] = acc_ref[u, h] * factor + update
        m_ref[u, h : h + 1, :] = top


STATE = (
    jax.ShapeDtypeStruct((2, 8, 2 * TOKENS), F32),
    jax.ShapeDtypeStruct((2, 8, 2 * TOKENS), F32),
    jax.ShapeDtypeStruct((2, HEADS // 4, HEAD_DIM, 2 * TOKENS), F32),
)
ITEM_FLOPS = 4 * 256 * 256 * 128 * 3


def attend_own(ids, mask_ref, q_ref, a_ref, b_ref, m_ref, l_ref, acc_ref):
    m_ref[...] = jnp.zeros_like(m_ref)
    l_ref[...] = jnp.zeros_like(l_ref)
    absorb(ids, mask_ref, q_ref, a_ref, m_ref, l_ref, acc_ref, 0, 0, 0, True)
    absorb(ids, mask_ref, q_ref, b_ref, m_ref, l_ref, acc_ref, 1, 0, 1, True)


def attend_pair(items, ids, mask_ref, q_ref, c0, c1, m_in, l_in, acc_in, m_ref, l_ref, acc_ref):
    m_ref[...] = m_in[...]
    l_ref[...] = l_in[...]
    acc_ref[...] = acc_in[...]
    for kv_ref, (source, delta, query) in zip((c0, c1), items):
        absorb(ids, mask_ref, q_ref, kv_ref, m_ref, l_ref, acc_ref, source, delta, query, False)


def attend_last(ids, mask_ref, q_ref, c0, c1, m_in, l_in, acc_in, *rest):
    outs, (m_ref, l_ref, acc_ref) = rest[:4], rest[4:]
    m_ref[...] = m_in[...]
    l_ref[...] = l_in[...]
    acc_ref[...] = acc_in[...]
    for u in range(2):
        for source, kv_ref in ((0, c0), (1, c1)):
            absorb(ids, mask_ref, q_ref, kv_ref, m_ref, l_ref, acc_ref, source, 4, u, False)
    for u in range(2):
        for h in range(GROUP // HEAD_DIM):
            out = acc_ref[u, h] / l_ref[u, h : h + 1, :]
            out = out.T.astype(BF16)
            cols = slice(h * HEAD_DIM, (h + 1) * HEAD_DIM)
            outs[2 * u][:, cols] = out[:TOKENS]
            outs[2 * u + 1][:, cols] = out[TOKENS:]


def scan_pack(x_ref, bc_ref, log_ref, out_ref):
    lanes = iota((TOKENS, WIN), 1)
    logs = log_ref[...]
    bc = bc_ref[...]
    head = iota((SCAN_HEADS, WIN), 0)
    lane = iota((SCAN_HEADS, WIN), 1)
    for s in range(N_SPACE):
        base = 384 * (s // 2) + 128 * (s % 2)
        free = 0 if s % 2 else 192
        pick = ((lane - free) == (head - 3 * s)) & (head >= 3 * s) & (head < 3 * s + 3)
        moved = dot(logs, jnp.where(pick, 1.0, 0.0).astype(BF16), (0, 0)).astype(BF16)
        window = x_ref[:, base : base + WIN]
        own = lanes >= 64 if s % 2 else lanes < 192
        out_ref[s, :, :WIN] = jnp.where(own, window, moved)
        out_ref[s, :, WIN:] = bc


def split_high(a):
    high = a.astype(BF16)
    return high, (a - high.astype(F32)).astype(BF16)


def scan_frame(ids, order_ref, in_ref, y_ref, row_ref, col_ref, state_ref, rows, cols):
    odd = ids[2] % 2
    free = jnp.where(odd == 1, 0, 192)
    for s in range(N_SPACE):
        for t in range(3):
            part = in_ref[s, :, t * 128 : (t + 1) * 128]
            rows[t, s * TOKENS : (s + 1) * TOKENS, :] = part.astype(F32)
    for k in range(COLS):
        for t in range(3):
            cols[t, k * 32 : (k + 1) * 32, :] = rows[t, pl.ds(order_ref[k], 32, stride=COLS), :]

    lane = iota((WIN, WIN), 1)
    spread = (iota((WIN, WIN), 0) == free + lane // 64 - odd) & (lane // 64 != free // 64)
    spread = jnp.where(spread, 1.0, 0.0).astype(BF16)
    wide = iota((WIN, 3 * TOKENS), 0) == free + iota((WIN, 3 * TOKENS), 1) // TOKENS
    wide = jnp.where(wide, 1.0, 0.0).astype(BF16)
    i, j = iota((TOKENS, TOKENS), 0), iota((TOKENS, TOKENS), 1)
    lower_mask = i >= j
    lower = jnp.where(lower_mask, 1.0, 0.0).astype(BF16)
    upper = jnp.where(i <= j, 1.0, 0.0).astype(BF16)
    group = iota((TOKENS, WIN), 1) // 64
    real = group != free // 64

    def block(buf, b, carry, before):
        start = pl.multiple_of(b * TOKENS, TOKENS)
        here = pl.ds(start, TOKENS)
        window = jnp.concatenate([buf[0, here, :], buf[1, here, :]], axis=1)
        bc = buf[2, here, :].astype(BF16)
        b_proj, c_proj = bc[:, :STATE_DIM], bc[:, STATE_DIM:]
        packed = window.astype(BF16)
        x = jnp.where(real, window, 0.0)
        log_lane = dot(packed, spread).astype(BF16)
        log_wide = dot(packed, wide).astype(BF16)
        cum = dot(lower, log_lane)
        cum_i = dot(lower, log_wide)
        scores = dot(c_proj, b_proj, (1, 1))
        mixers, parts = [], []
        for h in range(3):
            span = slice(h * TOKENS, (h + 1) * TOKENS)
            cum_j = dot(log_wide[:, span], upper, (0, 0))
            gap = jnp.where(lower_mask, cum_i[:, span] - cum_j, FLOOR)
            mixers.append((scores * jnp.exp(gap)).astype(BF16))
            parts.append(jnp.where(group == h + odd, x, 0.0).astype(BF16))
        inside = dot(jnp.concatenate(mixers, axis=1), jnp.concatenate(parts, axis=0))
        total = cum[TOKENS - 1 : TOKENS, :]
        local = dot(b_proj, (x * jnp.exp(total - cum)).astype(BF16), (0, 0))
        high, low = split_high(carry)
        carried = dot(c_proj, high) + dot(c_proj, low)
        out = inside + jnp.exp(cum) * carried
        return out, jnp.exp(cum + before), jnp.exp(total) * carry + local, before + total

    carry = jnp.zeros((STATE_DIM, WIN), F32)
    before = jnp.zeros((1, WIN), F32)

    def row_block(b, state):
        out, decay, carry, before = block(rows, b, *state)
        here = pl.ds(pl.multiple_of(b * TOKENS, TOKENS), TOKENS)
        for t in range(2):
            y_ref[t, here, :] = out[:, t * 128 : (t + 1) * 128]
            row_ref[t, here, :] = decay[:, t * 128 : (t + 1) * 128]
        return carry, before

    def col_block(b, state):
        out, decay, carry, before = block(cols, b, *state)
        for k in range(TOKENS // 32):
            here = pl.ds(order_ref[b * 4 + k], 32, stride=COLS)
            span = slice(k * 32, (k + 1) * 32)
            for t in range(2):
                lanes = slice(t * 128, (t + 1) * 128)
                y_ref[t, here, :] = y_ref[t, here, :] + out[span, lanes]
                col_ref[t, here, :] = decay[span, lanes]
        return carry, before

    for at, step in ((0, row_block), (ROWS, col_block)):
        end, whole = lax.fori_loop(0, N_SPACE, step, (carry, before))
        state_ref[at : at + STATE_DIM, :] = end
        state_ref[at + STATE_DIM : at + ROWS, :] = jnp.broadcast_to(whole, (8, WIN))


def scan_finish(ids, in_ref, y_ref, row_ref, col_ref, state_ref, gain_ref, out_ref):
    odd = ids[2] % 2
    same = iota((WIN, WIN), 0) // 64 == iota((WIN, WIN), 1) // 64
    same = jnp.where(same, 1.0, 0.0).astype(BF16)
    row_high, row_low = split_high(state_ref[:STATE_DIM, :])
    col_high, col_low = split_high(state_ref[ROWS : ROWS + STATE_DIM, :])
    gain = gain_ref[...]
    for s in range(N_SPACE):
        here = slice(s * TOKENS, (s + 1) * TOKENS)
        c_proj = in_ref[s][:, WIN + STATE_DIM :]
        y, row_decay, col_decay = (
            jnp.concatenate([ref[0, here, :], ref[1, here, :]], axis=1)
            for ref in (y_ref, row_ref, col_ref)
        )
        total = y + row_decay * (dot(c_proj, row_high) + dot(c_proj, row_low))
        total = total + col_decay * (dot(c_proj, col_high) + dot(c_proj, col_low))
        high, low = split_high(total * total)
        meansq = (dot(high, same) + dot(low, same)) * (1.0 / SCAN_DIM)
        normed = total * lax.rsqrt(meansq + EPS) * gain
        left, right = normed[:, :128], normed[:, 128:]
        full = jnp.where(odd == 1, right, left)
        part = jnp.where(odd == 1, left, right)
        out_ref[s, :TOKENS, :] = full.astype(BF16)
        out_ref[s, TOKENS:, :] = (part[:64] + pltpu.roll(part[64:], 64, 1)).astype(BF16)


def join(earlier, later):
    decay = jnp.exp(later[:, STATE_DIM : STATE_DIM + 1, :])
    states = jnp.arange(ROWS)[None, :, None] < STATE_DIM
    return jnp.where(states, decay, 1.0) * earlier + later


def states_before(own, frame):
    total = own
    before = jnp.zeros_like(own)
    for bit in (1, 2, 4, 8, 16):
        other = lax.ppermute(total, "tm", [(i, i ^ bit) for i in range(N_TM)])
        upper = (frame & bit) > 0
        before = jnp.where(upper, join(other, before), before)
        if bit < 16:
            total = jnp.where(upper, join(other, total), join(total, other))
    return before


def add_up(ids, scan_ref, *rest):
    group = ids[0]
    out_ref, total = rest[4], rest[5]
    low_half = iota((64, 128), 1) < 64
    for k in range(4):
        even, uneven = scan_ref[2 * k], scan_ref[2 * k + 1]
        e, o = even[TOKENS:].astype(F32), uneven[TOKENS:].astype(F32)
        total[:, 384 * k : 384 * k + 128] = even[:TOKENS].astype(F32)
        total[:64, 384 * k + 128 : 384 * k + 256] = jnp.where(low_half, e, o)
        total[64:, 384 * k + 128 : 384 * k + 256] = jnp.where(
            low_half, pltpu.roll(e, 64, 1), pltpu.roll(o, 64, 1)
        )
        total[:, 384 * k + 256 : 384 * k + 384] = uneven[:TOKENS].astype(F32)
    for i in range(4):
        cols = pl.ds(pl.multiple_of((group ^ i) * GROUP, 128), GROUP)
        out_ref[:, cols] = (total[:, cols] + rest[i][...].astype(F32)).astype(BF16)


def z_shift(array, by):
    pairs = []
    for half in range(2):
        for z in range(8):
            for core in range(2):
                pairs.append((16 * half + 2 * z + core, 16 * half + 2 * ((z + by) % 8) + core))
    return lax.ppermute(array, "tm", pairs)


def partner(array, bits):
    return lax.ppermute(array, "tm", [(i, i ^ bits) for i in range(N_TM)])


def on_device(queries, keys, values, tile_mask, inner_x, bc_proj, log_decay, col_order, norm_gain):
    frame = lax.axis_index("tm")
    tile = lax.axis_index("space")
    group = 2 * (frame // 16) + frame % 2
    ids = jnp.stack([group, (frame // 2) % 8, tile]).astype(jnp.int32)

    qkv = jax.ShapeDtypeStruct((3, TOKENS, GROUP), BF16)
    own, to_core, to_half, to_both = call(
        head_groups, (qkv,) * 4, 1, 3, moved=4 * 3 * TOKENS * HEADS * HEAD_DIM
    )(ids, queries, keys, values)
    from_core = partner(to_core, 1)
    chunk_a = jnp.stack([own[1:], from_core[1:]])

    sent = call(
        scan_pack, jax.ShapeDtypeStruct((N_SPACE, TOKENS, WIN + 128), BF16), 0, 3, moved=1 << 20
    )(inner_x, bc_proj, log_decay)
    frame_in = lax.all_to_all(sent, "space", split_axis=0, concat_axis=0, tiled=True)

    from_half = partner(to_half, 16)
    from_both = partner(to_both, 17)
    chunk_b = jnp.stack([from_half[1:], from_both[1:]])
    q_all = jnp.stack([own[0], from_core[0], from_half[0], from_both[0]])
    q_all = q_all.reshape(2, 2, TOKENS, GROUP)

    frame_tokens = N_SPACE * TOKENS
    wide = jax.ShapeDtypeStruct((2, frame_tokens, 128), F32)
    y, row_decay, col_decay, state = call(
        scan_frame,
        (wide, wide, wide, jax.ShapeDtypeStruct((2 * ROWS, WIN), F32)),
        2,
        1,
        scratch=[pltpu.VMEM((3, frame_tokens, 128), F32)] * 2,
        flops=1 << 30,
        moved=4 << 20,
    )(ids, col_order, frame_in)

    state = states_before(state.reshape(2, ROWS, WIN), frame).reshape(2 * ROWS, WIN)
    gain = lax.dynamic_slice(norm_gain, (384 * (tile // 2) + 128 * (tile % 2),), (WIN,))
    normed = call(
        scan_finish,
        jax.ShapeDtypeStruct((N_SPACE, 192, 128), BF16),
        1,
        6,
        flops=1 << 29,
        moved=4 << 20,
    )(ids, frame_in, y, row_decay, col_decay, state, gain.reshape(1, WIN))
    scan_rows = lax.all_to_all(normed, "space", split_axis=0, concat_axis=0, tiled=True)

    chunks = {(0, 0): chunk_a, (1, 0): chunk_b}
    flash = call(attend_own, STATE, 2, 3, flops=2 * ITEM_FLOPS, moved=4 << 20)(
        ids, tile_mask, q_all, chunk_a, chunk_b
    )
    for source, step in ((0, 1), (0, 2), (1, 1), (0, 3), (1, 2), (1, 3)):
        for sign in (1, -1):
            behind = chunks[source, sign * (step - 1)]
            chunks[source, sign * step] = z_shift(behind, -sign)
        items = ((source, step, None), (source, -step, None))
        flash = call(
            functools.partial(attend_pair, items), STATE, 2, 6, flops=2 * ITEM_FLOPS, moved=4 << 20
        )(ids, tile_mask, q_all, chunks[source, step], chunks[source, -step], *flash)
    far_a = z_shift(chunks[0, 3], -1)
    far_b = z_shift(chunks[1, -3], 1)
    piece = jax.ShapeDtypeStruct((TOKENS, GROUP), BF16)
    pieces = call(
        attend_last,
        (piece,) * 4,
        2,
        6,
        scratch=[pltpu.VMEM(s.shape, s.dtype) for s in STATE],
        flops=4 * ITEM_FLOPS,
        moved=4 << 20,
    )(ids, tile_mask, q_all, far_a, far_b, *flash)
    attention = (
        pieces[0],
        partner(pieces[1], 1),
        partner(pieces[2], 16),
        partner(pieces[3], 17),
    )
    return call(
        add_up,
        jax.ShapeDtypeStruct((TOKENS, HEADS * HEAD_DIM), BF16),
        1,
        5,
        scratch=[pltpu.VMEM((TOKENS, HEADS * HEAD_DIM), F32)],
        moved=2 << 20,
    )(ids, scan_rows, *attention)


def solution(mesh):
    return jax.shard_map(
        on_device,
        mesh=mesh,
        in_specs=(
            P(("tm", "space"), None),
            P(("tm", "space"), None),
            P(("tm", "space"), None),
            P(),
            P(("tm", "space"), None),
            P(("tm", "space"), None),
            P(None, ("tm", "space")),
            P(),
            P(),
        ),
        out_specs=P(("tm", "space"), None),
        check_vma=False,
    )
```

```python
import functools
import math

import jax
import jax.numpy as jnp
from jax import lax
from jax.experimental import pallas as pl
from jax.experimental.pallas import tpu as pltpu
from jax.sharding import PartitionSpec as P

HEADS = 12
HEAD_DIM = 128
SCAN_HEADS = 24
SCAN_DIM = 64
STATE_DIM = 64
COLS = 32
TOKENS = 128
N_TM = 32
N_SPACE = 8
GROUP = HEADS // 4 * HEAD_DIM
WIN = 256
ROWS = STATE_DIM + 8

EPS = 1e-05
FLOOR = -1e30
LOG2_SCALE = HEAD_DIM ** (-0.5) * math.log2(math.e)
BF16 = jnp.bfloat16
F32 = jnp.float32

VMEM = pl.BlockSpec(memory_space=pltpu.VMEM)
SMEM = pl.BlockSpec(memory_space=pltpu.SMEM)
ANY = pl.BlockSpec(memory_space=pl.ANY)


def call(body, out_shape, n_smem, n_vmem, us, scratch=(), space=VMEM):
    return pl.pallas_call(
        body,
        out_shape=out_shape,
        in_specs=[SMEM] * n_smem + [space] * n_vmem,
        out_specs=jax.tree.map(lambda _: space, out_shape),
        scratch_shapes=list(scratch),
        compiler_params=pltpu.CompilerParams(vmem_limit_bytes=24 * 2**20),
        cost_estimate=pl.CostEstimate(
            flops=int(us * 1.1e9), bytes_accessed=int(us * 3e6), transcendentals=0
        ),
    )


def dot(a, b, contract=(1, 0)):
    return lax.dot_general(
        a, b, (((contract[0],), (contract[1],)), ((), ())), preferred_element_type=F32
    )


def iota(shape, axis):
    return lax.broadcasted_iota(jnp.int32, shape, axis)


def head_groups(ids, q_ref, k_ref, v_ref, *rest):
    outs, sems = rest[:4], rest[4]
    copies = []
    for i in (1, 0, 2, 3):
        cols = pl.ds(pl.multiple_of((ids[0] ^ i) * GROUP, 128), GROUP)
        for t, ref in enumerate((q_ref, k_ref, v_ref)):
            copies.append(pltpu.make_async_copy(ref.at[:, cols], outs[i].at[t], sems.at[i, t]))
    for copy in copies:
        copy.start()
    for copy in copies:
        copy.wait()


STATE = (
    jax.ShapeDtypeStruct((2, 8, 2 * TOKENS), F32),
    jax.ShapeDtypeStruct((2, 8, 2 * TOKENS), F32),
    jax.ShapeDtypeStruct((2, HEADS // 4, HEAD_DIM, 2 * TOKENS), F32),
)


def absorb(ids, mask_ref, q_ref, u, sources, state):
    group, place = ids[0], ids[1]
    half, core = group // 2, group % 2
    lanes = iota((1, 2 * TOKENS), 1)
    biases = []
    for _, half_k, place_k in sources:
        for j in range(2):
            frame_k = 16 * half_k + 2 * place_k + (core ^ j)
            seen = [
                jnp.where(mask_ref[16 * (half ^ u) + 2 * place + (core ^ a), frame_k] > 0, 0.0, FLOOR)
                for a in range(2)
            ]
            biases.append(jnp.where(lanes < TOKENS, seen[0], seen[1]).astype(F32))
    new = []
    for h in range(GROUP // HEAD_DIM):
        cols = slice(h * HEAD_DIM, (h + 1) * HEAD_DIM)
        q = q_ref[u, :, :, cols].reshape(2 * TOKENS, HEAD_DIM)
        k = jnp.concatenate([load(0, cols) for load, _, _ in sources], axis=0)
        v = jnp.concatenate([load(1, cols) for load, _, _ in sources], axis=0)
        scores = dot(k, q, (1, 1))
        parts = [scores[i * TOKENS : (i + 1) * TOKENS] for i in range(len(biases))]
        tops = [
            jnp.max(s, axis=0, keepdims=True) * LOG2_SCALE + bias for s, bias in zip(parts, biases)
        ]
        top = functools.reduce(jnp.maximum, tops)
        if state is not None:
            old, total_in, acc_in = state[h]
            top = jnp.maximum(top, old)
        probs = [jnp.exp2(s * LOG2_SCALE + (bias - top)) for s, bias in zip(parts, biases)]
        total = jnp.sum(functools.reduce(jnp.add, probs), axis=0, keepdims=True)
        update = dot(v, jnp.concatenate([p.astype(BF16) for p in probs], axis=0), (0, 0))
        if state is not None:
            factor = jnp.exp2(old - top)
            total = total_in * factor + total
            update = acc_in * factor + update
        new.append((top, total, update))
    return new


def loader(ref):
    return lambda t, cols: ref[:, t, :, cols].reshape(2 * TOKENS, HEAD_DIM)


def either(first, a_ref, b_ref):
    a, b = loader(a_ref), loader(b_ref)
    return lambda t, cols: jnp.where(first, a(t, cols), b(t, cols))


def read_state(u, m_ref, l_ref, acc_ref):
    return [
        (m_ref[u, h : h + 1, :], l_ref[u, h : h + 1, :], acc_ref[u, h])
        for h in range(GROUP // HEAD_DIM)
    ]


def write_state(u, new, m_ref, l_ref, acc_ref):
    for h, (top, total, acc) in enumerate(new):
        m_ref[u, h : h + 1, :] = top
        l_ref[u, h : h + 1, :] = total
        acc_ref[u, h] = acc
    rest = jnp.zeros((8 - len(new), 2 * TOKENS), F32)
    m_ref[u, len(new) :, :] = rest
    l_ref[u, len(new) :, :] = rest


def attend_own(ids, mask_ref, q_ref, a_ref, b_ref, *state_out):
    half = ids[0] // 2
    for u, ref in enumerate((a_ref, b_ref)):
        new = absorb(ids, mask_ref, q_ref, u, [(loader(ref), half ^ u, ids[1])], None)
        write_state(u, new, *state_out)


def attend_step(step, ids, mask_ref, q_ref, a_up, a_down, b_up, b_down, *states):
    half, place = ids[0] // 2, ids[1]
    above, below = place + step, place - step
    for u in range(2):
        flip_up, flip_down = u ^ (above // 8), u ^ jnp.where(below < 0, 1, 0)
        sources = [
            (either(flip_up == 0, a_up, b_up), half ^ flip_up, above % 8),
            (either(flip_down == 0, a_down, b_down), half ^ flip_down, (below + 8) % 8),
        ]
        new = absorb(ids, mask_ref, q_ref, u, sources, read_state(u, *states[:3]))
        write_state(u, new, *states[3:])


def attend_last(ids, mask_ref, q_ref, a_ref, b_ref, m_in, l_in, acc_in, *outs):
    half, far = ids[0] // 2, (ids[1] + 4) % 8
    sources = [(loader(a_ref), half, far), (loader(b_ref), half ^ 1, far)]
    for u in range(2):
        state = read_state(u, m_in, l_in, acc_in)
        for h, (_, total, acc) in enumerate(absorb(ids, mask_ref, q_ref, u, sources, state)):
            out = (acc / total).T.astype(BF16)
            cols = slice(h * HEAD_DIM, (h + 1) * HEAD_DIM)
            outs[2 * u][:, cols] = out[:TOKENS]
            outs[2 * u + 1][:, cols] = out[TOKENS:]


def scan_pack(x_ref, bc_ref, log_ref, out_ref):
    lanes = iota((TOKENS, WIN), 1)
    logs = log_ref[...]
    bc = bc_ref[...]
    head = iota((SCAN_HEADS, WIN), 0)
    lane = iota((SCAN_HEADS, WIN), 1)
    for s in range(N_SPACE):
        base = 384 * (s // 2) + 128 * (s % 2)
        free = 0 if s % 2 else 192
        pick = ((lane - free) == (head - 3 * s)) & (head >= 3 * s) & (head < 3 * s + 3)
        moved = dot(logs, jnp.where(pick, 1.0, 0.0).astype(BF16), (0, 0)).astype(BF16)
        window = x_ref[:, base : base + WIN]
        own = lanes >= 64 if s % 2 else lanes < 192
        out_ref[s, :, :WIN] = jnp.where(own, window, moved)
        out_ref[s, :, WIN:] = bc


def split_high(a):
    high = a.astype(BF16)
    return high, (a - high.astype(F32)).astype(BF16)


def window_maps(ids):
    odd = ids[2] % 2
    free = jnp.where(odd == 1, 0, 192)
    lane = iota((WIN, WIN), 1)
    spread = (iota((WIN, WIN), 0) == free + lane // 64 - odd) & (lane // 64 != free // 64)
    group = iota((TOKENS, WIN), 1) // 64
    return odd, free, jnp.where(spread, 1.0, 0.0).astype(BF16), group


def lower_ones():
    return jnp.where(iota((TOKENS, TOKENS), 0) >= iota((TOKENS, TOKENS), 1), 1.0, 0.0).astype(BF16)


def scan_state(ids, order_ref, in_ref, row_ref, col_ref, state_ref, logs, moved):
    _, free, spread, group = window_maps(ids)
    lower = lower_ones()
    real = group != free // 64
    tiles = [slice(t * 128, (t + 1) * 128) for t in range(2)]
    spans = [slice(s * TOKENS, (s + 1) * TOKENS) for s in range(N_SPACE)]

    row_total = jnp.zeros((1, WIN), F32)
    for s, span in enumerate(spans):
        log = dot(in_ref[s, :, :WIN], spread)
        cum = dot(lower, log.astype(BF16)) + row_total
        row_total = cum[TOKENS - 1 :]
        for t, tile in enumerate(tiles):
            logs[t, span, :] = log[:, tile]
            row_ref[t, span, :] = cum[:, tile]
    for k in range(COLS):
        for t in range(2):
            moved[t, k * 32 : (k + 1) * 32, :] = logs[t, pl.ds(order_ref[k], 32, stride=COLS), :]
    col_total = jnp.zeros((1, WIN), F32)
    for b, span in enumerate(spans):
        log = jnp.concatenate([moved[t, span, :] for t in range(2)], axis=1)
        cum = dot(lower, log.astype(BF16)) + col_total
        col_total = cum[TOKENS - 1 :]
        for k in range(4):
            for t, tile in enumerate(tiles):
                here = pl.ds(order_ref[b * 4 + k], 32, stride=COLS)
                col_ref[t, here, :] = cum[k * 32 : (k + 1) * 32, tile]
    for at, ref, total in ((0, row_ref, row_total), (ROWS, col_ref, col_total)):
        state = jnp.zeros((STATE_DIM, WIN), F32)
        for s, span in enumerate(spans):
            x = jnp.where(real, in_ref[s, :, :WIN].astype(F32), 0.0)
            cum = jnp.concatenate([ref[t, span, :] for t in range(2)], axis=1)
            kept = (x * jnp.exp(total - cum)).astype(BF16)
            state = state + dot(in_ref[s, :, WIN : WIN + STATE_DIM], kept, (0, 0))
        state_ref[at : at + STATE_DIM, :] = state
        state_ref[at + STATE_DIM : at + ROWS, :] = jnp.broadcast_to(total, (8, WIN))


def scan_inside(ids, order_ref, in_ref, y_ref, rows, cols):
    odd, free, spread, group = window_maps(ids)
    real = group != free // 64
    for s in range(N_SPACE):
        for t in range(3):
            part = in_ref[s, :, t * 128 : (t + 1) * 128]
            rows[t, s * TOKENS : (s + 1) * TOKENS, :] = part.astype(F32)
    for k in range(COLS):
        for t in range(3):
            cols[t, k * 32 : (k + 1) * 32, :] = rows[t, pl.ds(order_ref[k], 32, stride=COLS), :]

    wide = iota((WIN, 3 * TOKENS), 0) == free + iota((WIN, 3 * TOKENS), 1) // TOKENS
    wide = jnp.where(wide, 1.0, 0.0).astype(BF16)
    pick = (iota((8, WIN), 1) == free + iota((8, WIN), 0)) & (iota((8, WIN), 0) < 3)
    pick = jnp.where(pick, 1.0, 0.0).astype(BF16)
    i, j = iota((TOKENS, TOKENS), 0), iota((TOKENS, TOKENS), 1)
    lower_mask = i >= j
    lower = lower_ones()
    upper = jnp.where(i <= j, 1.0, 0.0).astype(BF16)

    def block(buf, b, carry):
        here = slice(b * TOKENS, (b + 1) * TOKENS)
        window = jnp.concatenate([buf[0, here, :], buf[1, here, :]], axis=1)
        bc = buf[2, here, :].astype(BF16)
        b_proj, c_proj = bc[:, :STATE_DIM], bc[:, STATE_DIM:]
        packed = window.astype(BF16)
        x = jnp.where(real, window, 0.0)
        cum = dot(lower, dot(packed, spread).astype(BF16))
        cum_i = dot(lower, dot(packed, wide).astype(BF16))
        cum_j = dot(dot(pick, packed, (1, 1)).astype(BF16), upper)
        scores = dot(c_proj, b_proj, (1, 1))
        mixers, parts = [], []
        for h in range(3):
            gap = cum_i[:, h * TOKENS : (h + 1) * TOKENS] - cum_j[h : h + 1, :]
            mixers.append((scores * jnp.exp(jnp.where(lower_mask, gap, FLOOR))).astype(BF16))
            parts.append(jnp.where(group == h + odd, window, 0.0).astype(BF16))
        out = dot(jnp.concatenate(mixers, axis=1), jnp.concatenate(parts, axis=0))
        total = cum[TOKENS - 1 :, :]
        if carry is not None:
            high, low = split_high(carry)
            out = out + jnp.exp(cum) * (dot(c_proj, high) + dot(c_proj, low))
        if b < N_SPACE - 1:
            local = dot(b_proj, (x * jnp.exp(total - cum)).astype(BF16), (0, 0))
            carry = local if carry is None else jnp.exp(total) * carry + local
        return out, carry

    carry = None
    for b in range(N_SPACE):
        out, carry = block(rows, b, carry)
        for t in range(2):
            y_ref[t, b * TOKENS : (b + 1) * TOKENS, :] = out[:, t * 128 : (t + 1) * 128]
    carry = None
    for b in range(N_SPACE):
        out, carry = block(cols, b, carry)
        for k in range(TOKENS // 32):
            here = pl.ds(order_ref[b * 4 + k], 32, stride=COLS)
            for t in range(2):
                part = out[k * 32 : (k + 1) * 32, t * 128 : (t + 1) * 128]
                y_ref[t, here, :] = y_ref[t, here, :] + part


def scan_finish(ids, in_ref, y_ref, row_ref, col_ref, state_ref, gain_ref, out_ref):
    odd = ids[2] % 2
    same = iota((WIN, WIN), 0) // 64 == iota((WIN, WIN), 1) // 64
    same = jnp.where(same, 1.0, 0.0).astype(BF16)
    row_high, row_low = split_high(state_ref[0])
    col_high, col_low = split_high(state_ref[1])
    gain = gain_ref[...]
    for s in range(N_SPACE):
        here = slice(s * TOKENS, (s + 1) * TOKENS)
        c_proj = in_ref[s][:, WIN + STATE_DIM :]
        y, row_cum, col_cum = (
            jnp.concatenate([ref[0, here, :], ref[1, here, :]], axis=1)
            for ref in (y_ref, row_ref, col_ref)
        )
        row_decay, col_decay = jnp.exp(row_cum), jnp.exp(col_cum)
        total = y + row_decay * (dot(c_proj, row_high) + dot(c_proj, row_low))
        total = total + col_decay * (dot(c_proj, col_high) + dot(c_proj, col_low))
        high, low = split_high(total * total)
        meansq = (dot(high, same) + dot(low, same)) * (1.0 / SCAN_DIM)
        normed = total * lax.rsqrt(meansq + EPS) * gain
        left, right = normed[:, :128], normed[:, 128:]
        full = jnp.where(odd == 1, right, left)
        part = jnp.where(odd == 1, left, right)
        out_ref[s, :TOKENS, :] = full.astype(BF16)
        out_ref[s, TOKENS:, :] = (part[:64] + pltpu.roll(part[64:], 64, 1)).astype(BF16)


def join(earlier, later):
    return tuple(
        jnp.exp(later[1]) * a + b if i == 0 else a + b for i, (a, b) in enumerate(zip(earlier, later))
    )


def states_before(own, frame):
    total = own
    before = jax.tree.map(jnp.zeros_like, own)
    for bit in (1, 2, 4, 8, 16):
        high, low = split_high(total[1])
        sent = jnp.concatenate(
            [total[0].astype(BF16), jnp.broadcast_to(high, (2, 8, WIN)), jnp.broadcast_to(low, (2, 8, WIN))],
            axis=1,
        )
        got = lax.ppermute(sent, "tm", [(i, i ^ bit) for i in range(N_TM)]).astype(F32)
        at = STATE_DIM
        other = (got[:, :at], got[:, at : at + 1] + got[:, at + 8 : at + 9])
        upper = (frame & bit) > 0
        pick = functools.partial(jnp.where, upper)
        before = jax.tree.map(pick, join(other, before), before)
        if bit < 16:
            total = jax.tree.map(pick, join(other, total), join(total, other))
    return before[0]


def add_up(ids, scan_ref, *rest):
    group = ids[0]
    out_ref, total = rest[4], rest[5]
    low_half = iota((64, 128), 1) < 64
    for k in range(4):
        even, uneven = scan_ref[2 * k], scan_ref[2 * k + 1]
        e, o = even[TOKENS:].astype(F32), uneven[TOKENS:].astype(F32)
        total[:, 384 * k : 384 * k + 128] = even[:TOKENS].astype(F32)
        total[:64, 384 * k + 128 : 384 * k + 256] = jnp.where(low_half, e, o)
        total[64:, 384 * k + 128 : 384 * k + 256] = jnp.where(
            low_half, pltpu.roll(e, 64, 1), pltpu.roll(o, 64, 1)
        )
        total[:, 384 * k + 256 : 384 * k + 384] = uneven[:TOKENS].astype(F32)
    for i in range(4):
        cols = pl.ds(pl.multiple_of((group ^ i) * GROUP, 128), GROUP)
        out_ref[:, cols] = (total[:, cols] + rest[i][...].astype(F32)).astype(BF16)


def z_shift(array, by):
    pairs = []
    for half in range(2):
        for z in range(8):
            for core in range(2):
                pairs.append((16 * half + 2 * z + core, 16 * half + 2 * ((z + by) % 8) + core))
    return lax.ppermute(array, "tm", pairs)


def partner(array, bits):
    return lax.ppermute(array, "tm", [(i, i ^ bits) for i in range(N_TM)])


def on_device(queries, keys, values, tile_mask, inner_x, bc_proj, log_decay, col_order, norm_gain):
    frame = lax.axis_index("tm")
    tile = lax.axis_index("space")
    group = 2 * (frame // 16) + frame % 2
    ids = jnp.stack([group, (frame // 2) % 8, tile]).astype(jnp.int32)

    sent = call(
        scan_pack, jax.ShapeDtypeStruct((N_SPACE, TOKENS, WIN + 128), BF16), 0, 3, 1.2
    )(inner_x, bc_proj, log_decay)
    frame_in = lax.all_to_all(sent, "space", split_axis=0, concat_axis=0, tiled=True)

    qkv = jax.ShapeDtypeStruct((3, TOKENS, GROUP), BF16)
    own, to_core, to_half, to_both = call(
        head_groups, (qkv,) * 4, 1, 3, 1.5, [pltpu.SemaphoreType.DMA((4, 3))], ANY
    )(ids, queries, keys, values)
    from_core = partner(to_core, 1)
    from_half = partner(to_half, 16)
    from_both = partner(to_both, 17)
    chunk_a = jnp.stack([own[1:], from_core[1:]])
    chunk_b = jnp.stack([from_half[1:], from_both[1:]])
    q_all = jnp.stack([own[0], from_core[0], from_half[0], from_both[0]])
    q_all = q_all.reshape(2, 2, TOKENS, GROUP)

    frame_tokens = N_SPACE * TOKENS
    wide = jax.ShapeDtypeStruct((2, frame_tokens, 128), F32)
    row_cum, col_cum, state = call(
        scan_state,
        (wide, wide, jax.ShapeDtypeStruct((2 * ROWS, WIN), F32)),
        2,
        1,
        2.5,
        [pltpu.VMEM((2, frame_tokens, 128), F32)] * 2,
    )(ids, col_order, frame_in)
    state = state.reshape(2, ROWS, WIN)
    state = states_before((state[:, :STATE_DIM], state[:, STATE_DIM : STATE_DIM + 1]), frame)
    y = call(scan_inside, wide, 2, 1, 5, [pltpu.VMEM((3, frame_tokens, 128), F32)] * 2)(
        ids, col_order, frame_in
    )
    gain = lax.dynamic_slice(norm_gain, (384 * (tile // 2) + 128 * (tile % 2),), (WIN,))
    normed = call(scan_finish, jax.ShapeDtypeStruct((N_SPACE, 192, 128), BF16), 1, 6, 3)(
        ids, frame_in, y, row_cum, col_cum, state, gain.reshape(1, WIN)
    )
    scan_rows = lax.all_to_all(normed, "space", split_axis=0, concat_axis=0, tiled=True)

    chunks = {(0, 0): chunk_a, (1, 0): chunk_b}
    flash = call(attend_own, STATE, 2, 3, 2)(ids, tile_mask, q_all, chunk_a, chunk_b)
    for source, step in ((0, 1), (0, 2), (1, 1), (0, 3), (1, 2), (1, 3)):
        for sign in (1, -1):
            behind = chunks[source, sign * (step - 1)]
            chunks[source, sign * step] = z_shift(behind, -sign)
        if source == 1:
            flash = call(functools.partial(attend_step, step), STATE, 2, 8, 2.5)(
                ids,
                tile_mask,
                q_all,
                chunks[0, step],
                chunks[0, -step],
                chunks[1, step],
                chunks[1, -step],
                *flash,
            )
    far_a = z_shift(chunks[0, 3], -1)
    far_b = z_shift(chunks[1, -3], 1)
    piece = jax.ShapeDtypeStruct((TOKENS, GROUP), BF16)
    pieces = call(attend_last, (piece,) * 4, 2, 6, 3)(ids, tile_mask, q_all, far_a, far_b, *flash)
    attention = (
        pieces[0],
        partner(pieces[1], 1),
        partner(pieces[2], 16),
        partner(pieces[3], 17),
    )
    return call(
        add_up,
        jax.ShapeDtypeStruct((TOKENS, HEADS * HEAD_DIM), BF16),
        1,
        5,
        1.5,
        [pltpu.VMEM((TOKENS, HEADS * HEAD_DIM), F32)],
    )(ids, scan_rows, *attention)


def solution(mesh):
    return jax.shard_map(
        on_device,
        mesh=mesh,
        in_specs=(
            P(("tm", "space"), None),
            P(("tm", "space"), None),
            P(("tm", "space"), None),
            P(),
            P(("tm", "space"), None),
            P(("tm", "space"), None),
            P(None, ("tm", "space")),
            P(),
            P(),
        ),
        out_specs=P(("tm", "space"), None),
        check_vma=False,
    )
```

```python
import functools
import math

import jax
import jax.numpy as jnp
from jax import lax
from jax.experimental import pallas as pl
from jax.experimental.pallas import tpu as pltpu
from jax.sharding import PartitionSpec as P

HEADS = 12
HEAD_DIM = 128
SCAN_HEADS = 24
SCAN_DIM = 64
STATE_DIM = 64
COLS = 32
TOKENS = 128
N_TM = 32
N_SPACE = 8
GROUP = HEADS // 4 * HEAD_DIM
WIN = 256
ROWS = STATE_DIM + 8

COST = 0.1
EPS = 1e-05
FLOOR = -1e30
LOG2_SCALE = HEAD_DIM ** (-0.5) * math.log2(math.e)
BF16 = jnp.bfloat16
F32 = jnp.float32

VMEM = pl.BlockSpec(memory_space=pltpu.VMEM)
SMEM = pl.BlockSpec(memory_space=pltpu.SMEM)


def call(body, out_shape, n_smem, n_vmem, us, scratch=(), vmem=16):
    return pl.pallas_call(
        body,
        out_shape=out_shape,
        in_specs=[SMEM] * n_smem + [VMEM] * n_vmem,
        out_specs=jax.tree.map(lambda _: VMEM, out_shape),
        scratch_shapes=list(scratch),
        name=getattr(body, "func", body).__name__,
        compiler_params=pltpu.CompilerParams(vmem_limit_bytes=vmem * 2**20),
        cost_estimate=pl.CostEstimate(
            flops=int(us * 1.1e9 * COST), bytes_accessed=int(us * 3e6 * COST), transcendentals=0
        ),
    )


def dot(a, b, contract=(1, 0)):
    return lax.dot_general(
        a, b, (((contract[0],), (contract[1],)), ((), ())), preferred_element_type=F32
    )


def iota(shape, axis):
    return lax.broadcasted_iota(jnp.int32, shape, axis)


def head_groups(ids, q_ref, k_ref, v_ref, *outs):
    for i, out in enumerate(outs):
        cols = pl.ds(pl.multiple_of((ids[0] ^ i) * GROUP, 128), GROUP)
        for t, ref in enumerate((q_ref, k_ref, v_ref)):
            out[t] = ref[:, cols]


STATE = (
    jax.ShapeDtypeStruct((2, 8, 2 * TOKENS), F32),
    jax.ShapeDtypeStruct((2, 8, 2 * TOKENS), F32),
    jax.ShapeDtypeStruct((2, HEADS // 4, HEAD_DIM, 2 * TOKENS), F32),
)


def absorb(ids, mask_ref, q_ref, u, sources, state):
    group, place = ids[0], ids[1]
    half, core = group // 2, group % 2
    lanes = iota((1, 2 * TOKENS), 1)
    biases = []
    for _, half_k, place_k in sources:
        for j in range(2):
            frame_k = 16 * half_k + 2 * place_k + (core ^ j)
            seen = [
                jnp.where(mask_ref[16 * (half ^ u) + 2 * place + (core ^ a), frame_k] > 0, 0.0, FLOOR)
                for a in range(2)
            ]
            biases.append(jnp.where(lanes < TOKENS, seen[0], seen[1]).astype(F32))
    new = []
    for h in range(GROUP // HEAD_DIM):
        cols = slice(h * HEAD_DIM, (h + 1) * HEAD_DIM)
        q = q_ref[u, :, :, cols].reshape(2 * TOKENS, HEAD_DIM)
        k = jnp.concatenate([load(0, cols) for load, _, _ in sources], axis=0)
        v = jnp.concatenate([load(1, cols) for load, _, _ in sources], axis=0)
        scores = dot(k, q, (1, 1))
        parts = [scores[i * TOKENS : (i + 1) * TOKENS] for i in range(len(biases))]
        tops = [
            jnp.max(s, axis=0, keepdims=True) * LOG2_SCALE + bias for s, bias in zip(parts, biases)
        ]
        top = functools.reduce(jnp.maximum, tops)
        if state is not None:
            old, total_in, acc_in = state[h]
            top = jnp.maximum(top, old)
        probs = [jnp.exp2(s * LOG2_SCALE + (bias - top)) for s, bias in zip(parts, biases)]
        pb = jnp.concatenate([p.astype(BF16) for p in probs], axis=0); total = dot(jnp.ones((8, pb.shape[0]), BF16), pb)[:1]
        update = dot(v, pb, (0, 0))
        if state is not None:
            factor = jnp.exp2(old - top)
            total = total_in * factor + total
            update = acc_in * factor + update
        new.append((top, total, update))
    return new


def loader(ref):
    return lambda t, cols: ref[:, t, :, cols].reshape(2 * TOKENS, HEAD_DIM)


def either(first, a_ref, b_ref):
    a, b = loader(a_ref), loader(b_ref)
    return lambda t, cols: jnp.where(first, a(t, cols), b(t, cols))


def read_state(u, m_ref, l_ref, acc_ref):
    return [
        (m_ref[u, h : h + 1, :], l_ref[u, h : h + 1, :], acc_ref[u, h])
        for h in range(GROUP // HEAD_DIM)
    ]


def write_state(u, new, m_ref, l_ref, acc_ref):
    for h, (top, total, acc) in enumerate(new):
        m_ref[u, h : h + 1, :] = top
        l_ref[u, h : h + 1, :] = total
        acc_ref[u, h] = acc
    rest = jnp.zeros((8 - len(new), 2 * TOKENS), F32)
    m_ref[u, len(new) :, :] = rest
    l_ref[u, len(new) :, :] = rest


def attend_own(ids, mask_ref, own, core, other, both, m_ref, l_ref, acc_ref, q_out):
    half = ids[0] // 2
    for u, pair in enumerate(((own, core), (other, both))):
        q_out[u, 0], q_out[u, 1] = pair[0][0], pair[1][0]
    for u, (first, second) in enumerate(((own, core), (other, both))):

        def load(t, cols):
            return jnp.concatenate([first[t + 1, :, cols], second[t + 1, :, cols]], axis=0)

        new = absorb(ids, mask_ref, q_out, u, [(load, half ^ u, ids[1])], None)
        write_state(u, new, m_ref, l_ref, acc_ref)


def attend_step(step, ids, mask_ref, q_ref, a_up, a_down, b_up, b_down, *states):
    half, place = ids[0] // 2, ids[1]
    above, below = place + step, place - step
    for u in range(2):
        flip_up, flip_down = u ^ (above // 8), u ^ jnp.where(below < 0, 1, 0)
        sources = [
            (either(flip_up == 0, a_up, b_up), half ^ flip_up, above % 8),
            (either(flip_down == 0, a_down, b_down), half ^ flip_down, (below + 8) % 8),
        ]
        new = absorb(ids, mask_ref, q_ref, u, sources, read_state(u, *states[:3]))
        write_state(u, new, *states[3:])


def attend_last(u, ids, mask_ref, q_ref, a_ref, b_ref, m_in, l_in, acc_in, *outs):
    half, far = ids[0] // 2, (ids[1] + 4) % 8
    sources = [(loader(a_ref), half, far), (loader(b_ref), half ^ 1, far)]
    state = read_state(u, m_in, l_in, acc_in)
    for h, (_, total, acc) in enumerate(absorb(ids, mask_ref, q_ref, u, sources, state)):
        out = (acc / total).T.astype(BF16)
        cols = slice(h * HEAD_DIM, (h + 1) * HEAD_DIM)
        outs[0][:, cols] = out[:TOKENS]
        outs[1][:, cols] = out[TOKENS:]


def scan_pack(x_ref, bc_ref, log_ref, out_ref):
    lanes = iota((TOKENS, 128), 1)
    logs = log_ref[...].astype(F32)
    turned = pltpu.roll(logs, 64, 1)
    bc = bc_ref[...]
    for s in range(N_SPACE):
        base = 384 * (s // 2) + 128 * (s % 2)
        out_ref[s, :, :WIN] = x_ref[:, base : base + WIN]
        out_ref[s, :, WIN:] = bc
        heads, spun = logs[3 * s : 3 * s + 3], turned[3 * s : 3 * s + 3]
        rows = [heads, spun] if s % 2 else [spun, heads]
        rows = jnp.concatenate(rows + [jnp.zeros((10, 128), F32)], axis=0)
        at = slice(0, 128) if s % 2 else slice(128, 256)
        free = lanes[:16] < 64 if s % 2 else lanes[:16] >= 64
        out_ref[s, :16, at] = jnp.where(free, rows, out_ref[s, :16, at].astype(F32)).astype(BF16)


def split_high(a):
    high = a.astype(BF16)
    return high, (a - high.astype(F32)).astype(BF16)


def ones_where(condition):
    return jnp.where(condition, 1.0, 0.0).astype(BF16)


def log_rows(in_ref, odd):
    low = iota((8, 128), 1) < 64
    keep = iota((8, 128), 0) < 3
    tiles = []
    for s in range(N_SPACE):
        left, right = in_ref[s, :16, :128].astype(F32)[:8], in_ref[s, :16, 128:WIN].astype(F32)[:8]
        first = jnp.where(odd == 1, left, pltpu.roll(right, 64, 1))
        second = pltpu.roll(first, 64, 1)
        second = jnp.concatenate([second[3:], second[:3]], axis=0)
        tiles.append(jnp.where(keep, jnp.where(low, first, second), 0.0))
    return jnp.concatenate(tiles, axis=0).astype(BF16)


def stacked(rows, weights):
    out = dot(rows, weights)
    return [out[8 * s : 8 * s + 8] for s in range(N_SPACE)]


def running(parts):
    sums = [jnp.zeros_like(parts[0])]
    for part in parts:
        sums.append(sums[-1] + part)
    return sums[:-1], sums[-1]


def heads_diagonal(blocks, group, odd):
    return functools.reduce(
        jnp.add, [jnp.where(group == h + odd, block, 0.0) for h, block in enumerate(blocks)]
    )


def scan_state(ids, order_ref, in_ref, row_ref, col_ref, state_ref, sent_ref):
    odd = ids[2] % 2
    logs = log_rows(in_ref, odd)
    i, j = iota((TOKENS, TOKENS), 0), iota((TOKENS, TOKENS), 1)
    every = jnp.ones((TOKENS, TOKENS), BF16)
    row_before, total = running(stacked(logs, every))
    row_cum = [a + b for a, b in zip(stacked(logs, ones_where(i <= j)), row_before)]

    rank = jnp.zeros((TOKENS, TOKENS), F32)
    for k in range(COLS):
        rank = jnp.where(j % COLS == order_ref[k], float(k), rank)
    same_col = i % COLS == j % COLS
    earlier = stacked(logs, ones_where(rank.T < rank))
    earlier = functools.reduce(jnp.add, earlier)
    col_before, _ = running(stacked(logs, ones_where(same_col)))
    within = stacked(logs, ones_where(same_col & (i <= j)))
    col_cum = [a + b + earlier for a, b in zip(within, col_before)]

    group = iota((STATE_DIM, WIN), 1) // 64
    state = [jnp.zeros((STATE_DIM, WIN), F32)] * 6
    for s in range(N_SPACE):
        row_ref[s], col_ref[s] = row_cum[s], col_cum[s]
        b_turned = in_ref[s, :, WIN:].astype(F32).T[:STATE_DIM]
        lhs = []
        for cum in (row_cum[s], col_cum[s]):
            kept = jnp.exp(total - cum)
            lhs += [(b_turned * kept[h : h + 1]).astype(BF16) for h in range(3)]
        out = dot(jnp.concatenate(lhs, axis=0), in_ref[s, :, :WIN])
        state = [a + out[STATE_DIM * n : STATE_DIM * (n + 1)] for n, a in enumerate(state)]
    wide = jnp.concatenate([total, total], axis=1)
    lane_total = heads_diagonal(
        [jnp.broadcast_to(wide[h : h + 1], (8, WIN)) for h in range(3)], group[:8], odd
    )
    for n in range(2):
        at = n * ROWS
        own = heads_diagonal(state[3 * n : 3 * n + 3], group, odd)
        own = jnp.concatenate([own, lane_total], axis=0)
        state_ref[at : at + ROWS, :] = own
        sent_ref[n] = to_send(own)


def scan_inside(by_column, ids, order_ref, in_ref, *rest):
    odd = ids[2] % 2
    y_ref, buf = rest

    def strided(s, t):
        return in_ref[s, :, t * 128 : (t + 1) * 128].astype(F32)

    if by_column:
        rows, buf = buf.at[0], buf.at[1]
        for s in range(N_SPACE):
            for t in range(3):
                rows[t, s * TOKENS : (s + 1) * TOKENS, :] = strided(s, t)
        for k in range(COLS):
            for t in range(3):
                buf[t, k * 32 : (k + 1) * 32, :] = rows[t, pl.ds(order_ref[k], 32, stride=COLS), :]

    def load(b, t):
        return buf[t, b * TOKENS : (b + 1) * TOKENS, :] if by_column else strided(b, t)

    i, j = iota((TOKENS, TOKENS), 0), iota((TOKENS, TOKENS), 1)
    lower_mask = i >= j
    upper = ones_where(i <= j)
    every = jnp.ones((TOKENS, TOKENS), BF16)
    logs = log_rows(in_ref, odd)
    tile_of = (iota((8, TOKENS), 1) % 32) // 4
    col_logs = []
    for b in range(N_SPACE) if by_column else ():
        column = jnp.zeros((TOKENS, TOKENS), jnp.int32)
        for k in range(4):
            column = jnp.where(j // 32 == k, order_ref[4 * b + k], column)
        picked = stacked(logs, ones_where((i % COLS == column) & (i // COLS == j % 4)))
        log = jnp.zeros((8, TOKENS), F32)
        for s in range(N_SPACE):
            log = jnp.where(tile_of == s, picked[s], log)
        col_logs.append(log)
    if by_column:
        logs = jnp.concatenate(col_logs, axis=0).astype(BF16)

    group = iota((TOKENS, WIN), 1) // 64
    state_group = iota((STATE_DIM, WIN), 1) // 64

    def write_row(b, out):
        for t in range(2):
            y_ref[t, b * TOKENS : (b + 1) * TOKENS, :] = out[:, t * 128 : (t + 1) * 128]

    def write_col(b, out):
        for k in range(TOKENS // 32):
            here = pl.ds(order_ref[b * 4 + k], 32, stride=COLS)
            for t in range(2):
                part = out[k * 32 : (k + 1) * 32, t * 128 : (t + 1) * 128]
                y_ref[t, here, :] = part

    write = write_col if by_column else write_row
    carry = None
    cums, totals = stacked(logs, upper), stacked(logs, every)
    for b in range(N_SPACE):
        window = jnp.concatenate([load(b, 0), load(b, 1)], axis=1)
        bc = load(b, 2)
        turned, bc = bc.T, bc.astype(BF16)
        b_turned, c_turned = turned[:STATE_DIM], turned[STATE_DIM:]
        scores = dot(bc[:, STATE_DIM:], bc[:, :STATE_DIM], (1, 1))
        cum = cums[b]
        lhs, rhs = [], []
        for h in range(3):
            cum_j = jnp.broadcast_to(cum[h : h + 1], (TOKENS, TOKENS))
            gap = jnp.where(lower_mask, cum_j.T - cum_j, FLOOR)
            lhs.append((scores * jnp.exp(gap)).astype(BF16))
            rhs.append(jnp.where(group == h + odd, window, 0.0).astype(BF16))
        if carry is not None:
            decay = jnp.exp(cum)
            scaled = [c_turned * decay[h : h + 1] for h in range(3)]
            scaled.append(jnp.zeros_like(c_turned))
            scaled = jnp.concatenate(scaled, axis=0)
            lhs += [scaled[:128].T.astype(BF16), scaled[128:].T.astype(BF16)]
            for h in range(3):
                rhs.append(jnp.where(state_group == h + odd, carry[h], 0.0).astype(BF16))
            rhs.append(jnp.zeros((STATE_DIM, WIN), BF16))
        write(b, dot(jnp.concatenate(lhs, axis=1), jnp.concatenate(rhs, axis=0)))
        if b < N_SPACE - 1:
            kept = jnp.exp(totals[b] - cum)
            kept = [(b_turned * kept[h : h + 1]).astype(BF16) for h in range(3)]
            local = dot(jnp.concatenate(kept, axis=0), window.astype(BF16))
            local = [local[STATE_DIM * h : STATE_DIM * (h + 1)] for h in range(3)]
            if carry is not None:
                fade = jnp.exp(totals[b])
                fade = jnp.concatenate([fade, fade], axis=1)
                local = [a + fade[h : h + 1] * c for h, (a, c) in enumerate(zip(local, carry))]
            carry = local


def scan_finish(
    ids, in_ref, y_ref, z_ref, row_ref, col_ref, before_ref, swapped_ref, core_ref, gain_ref, out_ref
):
    odd = ids[2] % 2
    same = ones_where(iota((WIN, WIN), 0) // 64 == iota((WIN, WIN), 1) // 64)
    group = iota((STATE_DIM, WIN), 1) // 64
    core = ids[0] % 2
    states = []
    for n in range(2):
        state = jnp.where(core == n, before_ref[...].astype(F32), swapped_ref[...].astype(F32))
        first = from_sent(core_ref[n])
        decay = jnp.exp(first[STATE_DIM : STATE_DIM + 1])
        state = jnp.where(core == 1, decay * state + first[:STATE_DIM], state)
        states += [jnp.where(group == h + odd, state, 0.0).astype(BF16) for h in range(3)]
    states = jnp.concatenate(states, axis=0)
    gain = gain_ref[...]
    for s in range(N_SPACE):
        here = slice(s * TOKENS, (s + 1) * TOKENS)
        c_turned = in_ref[s, :, WIN:].astype(F32).T[STATE_DIM:]
        scaled = []
        for ref in (row_ref, col_ref):
            decay = jnp.exp(ref[s])
            scaled += [c_turned * decay[h : h + 1] for h in range(3)]
        scaled = [
            jnp.concatenate(scaled[2 * n : 2 * n + 2], axis=0).T.astype(BF16) for n in range(3)
        ]
        total = jnp.concatenate([y_ref[t, here, :] + z_ref[t, here, :] for t in range(2)], axis=1)
        total = total + dot(jnp.concatenate(scaled, axis=1), states)
        meansq = dot((total * total).astype(BF16), same) * (1.0 / SCAN_DIM)
        normed = total * lax.rsqrt(meansq + EPS) * gain
        left, right = normed[:, :128], normed[:, 128:]
        full = jnp.where(odd == 1, right, left)
        part = jnp.where(odd == 1, left, right)
        out_ref[s, :TOKENS, :] = full.astype(BF16)
        out_ref[s, TOKENS:, :] = (part[:64] + pltpu.roll(part[64:], 64, 1)).astype(BF16)


SENT = STATE_DIM + 16


def to_send(state):
    high, low = split_high(state[STATE_DIM:])
    return jnp.concatenate([state[:STATE_DIM].astype(BF16), high, low], axis=0)


def from_sent(sent):
    sent = sent.astype(F32)
    decay = sent[STATE_DIM : STATE_DIM + 8] + sent[STATE_DIM + 8 :]
    return jnp.concatenate([sent[:STATE_DIM], decay], axis=0)


def join(earlier, later):
    decay = jnp.exp(later[STATE_DIM : STATE_DIM + 1])
    return jnp.where(iota((ROWS, WIN), 0) < STATE_DIM, decay, 1.0) * earlier + later


def chip_state(ids, own_ref, got_ref, total_ref, sent_ref):
    core = ids[0] % 2
    at = pl.ds(pl.multiple_of(core * ROWS, 8), ROWS)
    own, other = own_ref[at, :], from_sent(got_ref[core])
    first = core == 0
    total = join(jnp.where(first, own, other), jnp.where(first, other, own))
    total_ref[...] = total
    sent_ref[...] = to_send(total)


def grow(bit, ids, got_ref, total_in, *rest):
    before_in, (before_ref, total_ref, sent_ref) = (rest[0], rest[1:]) if bit > 2 else (None, rest)
    other, total = from_sent(got_ref[...]), total_in[...]
    later = (ids[3] & bit) > 0
    before = other if before_in is None else join(other, before_in[...])
    before_ref[...] = jnp.where(later, before, 0.0 if before_in is None else before_in[...])
    total = join(jnp.where(later, other, total), jnp.where(later, total, other))
    total_ref[...] = total
    sent_ref[...] = to_send(total)


def last_before(ids, got_ref, before_in, sent_ref):
    before = before_in[...]
    before = jnp.where((ids[3] & 16) > 0, join(from_sent(got_ref[...]), before), before)
    sent_ref[...] = before[:STATE_DIM].astype(BF16)


def add_up(ids, scan_ref, *rest):
    group = ids[0]
    out_ref, total = rest[4], rest[5]
    low_half = iota((64, 128), 1) < 64
    for k in range(4):
        even, uneven = scan_ref[2 * k], scan_ref[2 * k + 1]
        e, o = even[TOKENS:].astype(F32), uneven[TOKENS:].astype(F32)
        total[:, 384 * k : 384 * k + 128] = even[:TOKENS].astype(F32)
        total[:64, 384 * k + 128 : 384 * k + 256] = jnp.where(low_half, e, o)
        total[64:, 384 * k + 128 : 384 * k + 256] = jnp.where(
            low_half, pltpu.roll(e, 64, 1), pltpu.roll(o, 64, 1)
        )
        total[:, 384 * k + 256 : 384 * k + 384] = uneven[:TOKENS].astype(F32)
    for i in range(4):
        cols = pl.ds(pl.multiple_of((group ^ i) * GROUP, 128), GROUP)
        out_ref[:, cols] = (total[:, cols] + rest[i][...].astype(F32)).astype(BF16)


def tie(*values):
    return lax.optimization_barrier(values)


def z_shift(array, by):
    pairs = []
    for half in range(2):
        for z in range(8):
            for core in range(2):
                pairs.append((16 * half + 2 * z + core, 16 * half + 2 * ((z + by) % 8) + core))
    return lax.ppermute(array, "tm", pairs)


def partner(array, bits):
    return lax.ppermute(array, "tm", [(i, i ^ bits) for i in range(N_TM)])


def on_device(queries, keys, values, tile_mask, inner_x, bc_proj, log_decay, col_order, norm_gain):
    frame = lax.axis_index("tm")
    tile = lax.axis_index("space")
    group = 2 * (frame // 16) + frame % 2
    ids = jnp.stack([group, (frame // 2) % 8, tile, frame]).astype(jnp.int32)

    qkv = jax.ShapeDtypeStruct((3, TOKENS, GROUP), BF16)
    own, to_core, to_half, to_both = call(
        head_groups, (qkv,) * 4, 1, 3, 1, vmem=56
    )(ids, queries, keys, values)
    from_core = partner(to_core, 1)
    from_half = partner(to_half, 16)
    from_both = partner(to_both, 17)
    chunks = {(0, 0): jnp.stack([own[1:], from_core[1:]])}
    inner_x, _ = tie(inner_x, chunks[0, 0])
    sent = call(
        scan_pack, jax.ShapeDtypeStruct((N_SPACE, TOKENS, WIN + 128), BF16), 0, 3, 1.5, vmem=56
    )(inner_x, bc_proj, log_decay)
    frame_in = lax.all_to_all(sent, "space", split_axis=0, concat_axis=0, tiled=True)


    def pass_on(source, step, after=None):
        if after is not None:
            behind, _ = tie(pair(source, step - 1), after)
            chunks[source, step - 1], chunks[source, 1 - step] = behind
        for sign in (1, -1):
            chunks[source, sign * step] = z_shift(chunks[source, sign * (step - 1)], -sign)

    def pair(source, step):
        return chunks[source, step], chunks[source, -step]

    def step_of(step, flash):
        return call(functools.partial(attend_step, step), STATE, 2, 8, 2.5)(
            ids, tile_mask, q_all, *pair(0, step), *pair(1, step), *flash
        )

    pass_on(0, 1)
    pass_on(0, 2)
    chunks[1, 0] = jnp.stack([from_half[1:], from_both[1:]])
    pass_on(1, 1)
    cum = jax.ShapeDtypeStruct((N_SPACE, 8, TOKENS), F32)
    one, sent = jax.ShapeDtypeStruct((ROWS, WIN), F32), jax.ShapeDtypeStruct((SENT, WIN), BF16)
    row_cum, col_cum, state, both_sent = call(
        scan_state,
        (
            cum,
            cum,
            jax.ShapeDtypeStruct((2 * ROWS, WIN), F32),
            jax.ShapeDtypeStruct((2, SENT, WIN), BF16),
        ),
        2,
        1,
        2,
    )(ids, col_order, frame_in)
    core_sent = partner(both_sent, 1)
    total, walk = call(chip_state, (one, sent), 1, 2, 0.5)(ids, state, core_sent)

    other = partner(walk, 2)
    own, _ = tie(own, walk)
    *flash, q_all = call(
        attend_own, STATE + (jax.ShapeDtypeStruct((2, 2, TOKENS, GROUP), BF16),), 2, 4, 2
    )(ids, tile_mask, own, from_core, from_half, from_both)
    other, flash = tie(other, flash)
    before, total, walk = call(functools.partial(grow, 2), (one, one, sent), 1, 2, 0.5)(
        ids, other, total
    )

    other = partner(walk, 4)
    frame_tokens = N_SPACE * TOKENS
    wide = jax.ShapeDtypeStruct((2, frame_tokens, 128), F32)
    pass_on(0, 3, walk)
    inside_in, _ = tie(frame_in, pair(1, 1))
    y_row = call(
        functools.partial(scan_inside, False), wide, 2, 1, 2, [pltpu.VMEM((8, 128), F32)]
    )(ids, col_order, inside_in)
    pass_on(1, 2, y_row)
    flash, y_row = tie(flash, y_row)
    flash = step_of(1, flash)
    other, flash, y_row = tie(other, flash, y_row)
    before, total, walk = call(functools.partial(grow, 4), (one, one, sent), 1, 3, 0.5)(
        ids, other, total, before
    )

    other = partner(walk, 8)
    pass_on(1, 3, walk)
    inside_in, _, _ = tie(inside_in, walk, pair(0, 3))
    y_col = call(
        functools.partial(scan_inside, True),
        wide,
        2,
        1,
        4,
        [pltpu.VMEM((2, 3, frame_tokens, 128), F32)],
    )(ids, col_order, inside_in)
    flash, y_col = tie(flash, y_col)
    flash = step_of(2, flash)
    other, flash, y_col = tie(other, flash, y_col)
    before, total, walk = call(functools.partial(grow, 8), (one, one, sent), 1, 3, 0.5)(
        ids, other, total, before
    )

    other = partner(walk, 16)
    (to_up, to_down), flash, walk = tie((chunks[0, 3], chunks[1, -3]), flash, walk)
    far_a, far_b = z_shift(to_up, -1), z_shift(to_down, 1)
    flash = step_of(3, flash)
    other, flash = tie(other, flash)
    before = call(last_before, jax.ShapeDtypeStruct((STATE_DIM, WIN), BF16), 1, 2, 0.5)(
        ids, other, before
    )
    before_other = partner(before, 1)

    gain = lax.dynamic_slice(norm_gain, (384 * (tile // 2) + 128 * (tile % 2),), (WIN,))
    normed = call(scan_finish, jax.ShapeDtypeStruct((N_SPACE, 192, 128), BF16), 1, 9, 3)(
        ids,
        frame_in,
        y_row,
        y_col,
        row_cum,
        col_cum,
        before,
        before_other,
        core_sent,
        gain.reshape(1, WIN),
    )
    scan_rows = lax.all_to_all(normed, "space", split_axis=0, concat_axis=0, tiled=True)
    flash, _ = tie(flash, normed)
    piece = jax.ShapeDtypeStruct((TOKENS, GROUP), BF16)
    pieces = {}
    for u in (1, 0):
        pieces[u] = call(functools.partial(attend_last, u), (piece, piece), 2, 6, 2)(
            ids, tile_mask, q_all, far_a, far_b, *flash
        )
        flash, pieces[u] = tie(flash, pieces[u])
    attention = (
        pieces[0][0],
        partner(pieces[0][1], 1),
        partner(pieces[1][0], 16),
        partner(pieces[1][1], 17),
    )
    return call(
        add_up,
        jax.ShapeDtypeStruct((TOKENS, HEADS * HEAD_DIM), BF16),
        1,
        5,
        1.5,
        [pltpu.VMEM((TOKENS, HEADS * HEAD_DIM), F32)],
    )(ids, scan_rows, *attention)


def solution(mesh):
    return jax.shard_map(
        on_device,
        mesh=mesh,
        in_specs=(
            P(("tm", "space"), None),
            P(("tm", "space"), None),
            P(("tm", "space"), None),
            P(),
            P(("tm", "space"), None),
            P(("tm", "space"), None),
            P(None, ("tm", "space")),
            P(),
            P(),
        ),
        out_specs=P(("tm", "space"), None),
        check_vma=False,
    )
```

```python
import functools
import math

import jax
import jax.numpy as jnp
from jax import lax
from jax.experimental import pallas as pl
from jax.experimental.pallas import tpu as pltpu
from jax.sharding import PartitionSpec as P

HEADS = 12
HEAD_DIM = 128
SCAN_HEADS = 24
SCAN_DIM = 64
STATE_DIM = 64
COLS = 32
TOKENS = 128
N_TM = 32
N_SPACE = 8
GROUP = HEADS // 4 * HEAD_DIM
WIN = 256
ROWS = STATE_DIM + 8

COST = 0.001
EPS = 1e-05
FLOOR = -1e30
LOG2_SCALE = HEAD_DIM ** (-0.5) * math.log2(math.e)
BF16 = jnp.bfloat16
F32 = jnp.float32

VMEM = pl.BlockSpec(memory_space=pltpu.VMEM)
SMEM = pl.BlockSpec(memory_space=pltpu.SMEM)


def call(body, out_shape, n_smem, n_vmem, us, scratch=(), vmem=16):
    return pl.pallas_call(
        body,
        out_shape=out_shape,
        in_specs=[SMEM] * n_smem + [VMEM] * n_vmem,
        out_specs=jax.tree.map(lambda _: VMEM, out_shape),
        scratch_shapes=list(scratch),
        name=getattr(body, "func", body).__name__,
        compiler_params=pltpu.CompilerParams(vmem_limit_bytes=vmem * 2**20),
        cost_estimate=pl.CostEstimate(
            flops=int(us * 1.1e9 * COST), bytes_accessed=int(us * 3e6 * COST), transcendentals=0
        ),
    )


def dot(a, b, contract=(1, 0)):
    return lax.dot_general(
        a, b, (((contract[0],), (contract[1],)), ((), ())), preferred_element_type=F32
    )


def iota(shape, axis):
    return lax.broadcasted_iota(jnp.int32, shape, axis)


def head_groups(ids, q_ref, k_ref, v_ref, *outs):
    for i, out in enumerate(outs):
        cols = pl.ds(pl.multiple_of((ids[0] ^ i) * GROUP, 128), GROUP)
        for t, ref in enumerate((q_ref, k_ref, v_ref)):
            out[t] = ref[:, cols]


STATE = (
    jax.ShapeDtypeStruct((2, 8, 2 * TOKENS), F32),
    jax.ShapeDtypeStruct((2, 8, 2 * TOKENS), F32),
    jax.ShapeDtypeStruct((2, HEADS // 4, HEAD_DIM, 2 * TOKENS), F32),
)


def absorb(ids, mask_ref, q_ref, u, sources, state):
    group, place = ids[0], ids[1]
    half, core = group // 2, group % 2
    lanes = iota((1, 2 * TOKENS), 1)
    biases = []
    for _, half_k, place_k in sources:
        for j in range(2):
            frame_k = 16 * half_k + 2 * place_k + (core ^ j)
            seen = [
                jnp.where(mask_ref[16 * (half ^ u) + 2 * place + (core ^ a), frame_k] > 0, 0.0, FLOOR)
                for a in range(2)
            ]
            biases.append(jnp.where(lanes < TOKENS, seen[0], seen[1]).astype(F32))
    new = []
    for h in range(GROUP // HEAD_DIM):
        cols = slice(h * HEAD_DIM, (h + 1) * HEAD_DIM)
        q = q_ref[u, :, :, cols].reshape(2 * TOKENS, HEAD_DIM)
        k = jnp.concatenate([load(0, cols) for load, _, _ in sources], axis=0)
        v = jnp.concatenate([load(1, cols) for load, _, _ in sources], axis=0)
        scores = dot(k, q, (1, 1))
        parts = [scores[i * TOKENS : (i + 1) * TOKENS] for i in range(len(biases))]
        tops = [
            jnp.max(s, axis=0, keepdims=True) * LOG2_SCALE + bias for s, bias in zip(parts, biases)
        ]
        top = functools.reduce(jnp.maximum, tops)
        if state is not None:
            old, total_in, acc_in = state[h]
            top = jnp.maximum(top, old)
        probs = [jnp.exp2(s * LOG2_SCALE + (bias - top)) for s, bias in zip(parts, biases)]
        pb = jnp.concatenate([p.astype(BF16) for p in probs], axis=0); total = dot(jnp.ones((8, pb.shape[0]), BF16), pb)[:1]
        update = dot(v, pb, (0, 0))
        if state is not None:
            factor = jnp.exp2(old - top)
            total = total_in * factor + total
            update = acc_in * factor + update
        new.append((top, total, update))
    return new


def loader(ref):
    return lambda t, cols: ref[:, t, :, cols].reshape(2 * TOKENS, HEAD_DIM)


def either(first, a_ref, b_ref):
    a, b = loader(a_ref), loader(b_ref)
    return lambda t, cols: jnp.where(first, a(t, cols), b(t, cols))


def read_state(u, m_ref, l_ref, acc_ref):
    return [
        (m_ref[u, h : h + 1, :], l_ref[u, h : h + 1, :], acc_ref[u, h])
        for h in range(GROUP // HEAD_DIM)
    ]


def write_state(u, new, m_ref, l_ref, acc_ref):
    for h, (top, total, acc) in enumerate(new):
        m_ref[u, h : h + 1, :] = top
        l_ref[u, h : h + 1, :] = total
        acc_ref[u, h] = acc
    rest = jnp.zeros((8 - len(new), 2 * TOKENS), F32)
    m_ref[u, len(new) :, :] = rest
    l_ref[u, len(new) :, :] = rest


def attend_own(ids, mask_ref, own, core, other, both, m_ref, l_ref, acc_ref, q_out):
    half = ids[0] // 2
    for u, pair in enumerate(((own, core), (other, both))):
        q_out[u, 0], q_out[u, 1] = pair[0][0], pair[1][0]
    for u, (first, second) in enumerate(((own, core), (other, both))):

        def load(t, cols):
            return jnp.concatenate([first[t + 1, :, cols], second[t + 1, :, cols]], axis=0)

        new = absorb(ids, mask_ref, q_out, u, [(load, half ^ u, ids[1])], None)
        write_state(u, new, m_ref, l_ref, acc_ref)


def attend_step(step, ids, mask_ref, q_ref, a_up, a_down, b_up, b_down, *states):
    half, place = ids[0] // 2, ids[1]
    above, below = place + step, place - step
    for u in range(2):
        flip_up, flip_down = u ^ (above // 8), u ^ jnp.where(below < 0, 1, 0)
        sources = [
            (either(flip_up == 0, a_up, b_up), half ^ flip_up, above % 8),
            (either(flip_down == 0, a_down, b_down), half ^ flip_down, (below + 8) % 8),
        ]
        new = absorb(ids, mask_ref, q_ref, u, sources, read_state(u, *states[:3]))
        write_state(u, new, *states[3:])


def attend_last(u, ids, mask_ref, q_ref, a_ref, b_ref, m_in, l_in, acc_in, *outs):
    half, far = ids[0] // 2, (ids[1] + 4) % 8
    sources = [(loader(a_ref), half, far), (loader(b_ref), half ^ 1, far)]
    state = read_state(u, m_in, l_in, acc_in)
    for h, (_, total, acc) in enumerate(absorb(ids, mask_ref, q_ref, u, sources, state)):
        out = (acc / total).T.astype(BF16)
        cols = slice(h * HEAD_DIM, (h + 1) * HEAD_DIM)
        outs[0][:, cols] = out[:TOKENS]
        outs[1][:, cols] = out[TOKENS:]


def scan_pack(x_ref, bc_ref, log_ref, out_ref):
    lanes = iota((TOKENS, 128), 1)
    logs = log_ref[...].astype(F32)
    turned = pltpu.roll(logs, 64, 1)
    bc = bc_ref[...]
    for s in range(N_SPACE):
        base = 384 * (s // 2) + 128 * (s % 2)
        out_ref[s, :, :WIN] = x_ref[:, base : base + WIN]
        out_ref[s, :, WIN:] = bc
        heads, spun = logs[3 * s : 3 * s + 3], turned[3 * s : 3 * s + 3]
        rows = [heads, spun] if s % 2 else [spun, heads]
        rows = jnp.concatenate(rows + [jnp.zeros((10, 128), F32)], axis=0)
        at = slice(0, 128) if s % 2 else slice(128, 256)
        free = lanes[:16] < 64 if s % 2 else lanes[:16] >= 64
        out_ref[s, :16, at] = jnp.where(free, rows, out_ref[s, :16, at].astype(F32)).astype(BF16)


def split_high(a):
    high = a.astype(BF16)
    return high, (a - high.astype(F32)).astype(BF16)


def ones_where(condition):
    return jnp.where(condition, 1.0, 0.0).astype(BF16)


def log_rows(in_ref, odd):
    low = iota((8, 128), 1) < 64
    keep = iota((8, 128), 0) < 3
    tiles = []
    for s in range(N_SPACE):
        left, right = in_ref[s, :16, :128].astype(F32)[:8], in_ref[s, :16, 128:WIN].astype(F32)[:8]
        first = jnp.where(odd == 1, left, pltpu.roll(right, 64, 1))
        second = pltpu.roll(first, 64, 1)
        second = jnp.concatenate([second[3:], second[:3]], axis=0)
        tiles.append(jnp.where(keep, jnp.where(low, first, second), 0.0))
    return jnp.concatenate(tiles, axis=0).astype(BF16)


def stacked(rows, weights):
    out = dot(rows, weights)
    return [out[8 * s : 8 * s + 8] for s in range(N_SPACE)]


def running(parts):
    sums = [jnp.zeros_like(parts[0])]
    for part in parts:
        sums.append(sums[-1] + part)
    return sums[:-1], sums[-1]


def heads_diagonal(blocks, group, odd):
    return functools.reduce(
        jnp.add, [jnp.where(group == h + odd, block, 0.0) for h, block in enumerate(blocks)]
    )


def scan_state(ids, order_ref, in_ref, row_ref, col_ref, state_ref, sent_ref):
    odd = ids[2] % 2
    logs = log_rows(in_ref, odd)
    i, j = iota((TOKENS, TOKENS), 0), iota((TOKENS, TOKENS), 1)
    every = jnp.ones((TOKENS, TOKENS), BF16)
    row_before, total = running(stacked(logs, every))
    row_cum = [a + b for a, b in zip(stacked(logs, ones_where(i <= j)), row_before)]

    rank = jnp.zeros((TOKENS, TOKENS), F32)
    for k in range(COLS):
        rank = jnp.where(j % COLS == order_ref[k], float(k), rank)
    same_col = i % COLS == j % COLS
    earlier = stacked(logs, ones_where(rank.T < rank))
    earlier = functools.reduce(jnp.add, earlier)
    col_before, _ = running(stacked(logs, ones_where(same_col)))
    within = stacked(logs, ones_where(same_col & (i <= j)))
    col_cum = [a + b + earlier for a, b in zip(within, col_before)]

    group = iota((STATE_DIM, WIN), 1) // 64
    state = [jnp.zeros((STATE_DIM, WIN), F32)] * 6
    for s in range(N_SPACE):
        row_ref[s], col_ref[s] = row_cum[s], col_cum[s]
        b_turned = in_ref[s, :, WIN:].astype(F32).T[:STATE_DIM]
        lhs = []
        for cum in (row_cum[s], col_cum[s]):
            kept = jnp.exp(total - cum)
            lhs += [(b_turned * kept[h : h + 1]).astype(BF16) for h in range(3)]
        out = dot(jnp.concatenate(lhs, axis=0), in_ref[s, :, :WIN])
        state = [a + out[STATE_DIM * n : STATE_DIM * (n + 1)] for n, a in enumerate(state)]
    wide = jnp.concatenate([total, total], axis=1)
    lane_total = heads_diagonal(
        [jnp.broadcast_to(wide[h : h + 1], (8, WIN)) for h in range(3)], group[:8], odd
    )
    for n in range(2):
        at = n * ROWS
        own = heads_diagonal(state[3 * n : 3 * n + 3], group, odd)
        own = jnp.concatenate([own, lane_total], axis=0)
        state_ref[at : at + ROWS, :] = own
        sent_ref[n] = to_send(own)


def scan_inside(by_column, ids, order_ref, in_ref, *rest):
    odd = ids[2] % 2
    y_ref, buf = rest

    def strided(s, t):
        return in_ref[s, :, t * 128 : (t + 1) * 128].astype(F32)

    if by_column:
        rows, buf = buf.at[0], buf.at[1]
        for s in range(N_SPACE):
            for t in range(3):
                rows[t, s * TOKENS : (s + 1) * TOKENS, :] = strided(s, t)
        for k in range(COLS):
            for t in range(3):
                buf[t, k * 32 : (k + 1) * 32, :] = rows[t, pl.ds(order_ref[k], 32, stride=COLS), :]

    def load(b, t):
        return buf[t, b * TOKENS : (b + 1) * TOKENS, :] if by_column else strided(b, t)

    i, j = iota((TOKENS, TOKENS), 0), iota((TOKENS, TOKENS), 1)
    lower_mask = i >= j
    upper = ones_where(i <= j)
    every = jnp.ones((TOKENS, TOKENS), BF16)
    logs = log_rows(in_ref, odd)
    tile_of = (iota((8, TOKENS), 1) % 32) // 4
    col_logs = []
    for b in range(N_SPACE) if by_column else ():
        column = jnp.zeros((TOKENS, TOKENS), jnp.int32)
        for k in range(4):
            column = jnp.where(j // 32 == k, order_ref[4 * b + k], column)
        picked = stacked(logs, ones_where((i % COLS == column) & (i // COLS == j % 4)))
        log = jnp.zeros((8, TOKENS), F32)
        for s in range(N_SPACE):
            log = jnp.where(tile_of == s, picked[s], log)
        col_logs.append(log)
    if by_column:
        logs = jnp.concatenate(col_logs, axis=0).astype(BF16)

    group = iota((TOKENS, WIN), 1) // 64
    state_group = iota((STATE_DIM, WIN), 1) // 64

    def write_row(b, out):
        for t in range(2):
            y_ref[t, b * TOKENS : (b + 1) * TOKENS, :] = out[:, t * 128 : (t + 1) * 128]

    def write_col(b, out):
        for k in range(TOKENS // 32):
            here = pl.ds(order_ref[b * 4 + k], 32, stride=COLS)
            for t in range(2):
                part = out[k * 32 : (k + 1) * 32, t * 128 : (t + 1) * 128]
                y_ref[t, here, :] = part

    write = write_col if by_column else write_row
    carry = None
    cums, totals = stacked(logs, upper), stacked(logs, every)
    for b in range(N_SPACE):
        window = jnp.concatenate([load(b, 0), load(b, 1)], axis=1)
        bc = load(b, 2)
        turned, bc = bc.T, bc.astype(BF16)
        b_turned, c_turned = turned[:STATE_DIM], turned[STATE_DIM:]
        scores = dot(bc[:, STATE_DIM:], bc[:, :STATE_DIM], (1, 1))
        cum = cums[b]
        lhs, rhs = [], []
        for h in range(3):
            cum_j = jnp.broadcast_to(cum[h : h + 1], (TOKENS, TOKENS))
            gap = jnp.where(lower_mask, cum_j.T - cum_j, FLOOR)
            lhs.append((scores * jnp.exp(gap)).astype(BF16))
            rhs.append(jnp.where(group == h + odd, window, 0.0).astype(BF16))
        if carry is not None:
            decay = jnp.exp(cum)
            scaled = [c_turned * decay[h : h + 1] for h in range(3)]
            scaled.append(jnp.zeros_like(c_turned))
            scaled = jnp.concatenate(scaled, axis=0)
            lhs += [scaled[:128].T.astype(BF16), scaled[128:].T.astype(BF16)]
            for h in range(3):
                rhs.append(jnp.where(state_group == h + odd, carry[h], 0.0).astype(BF16))
            rhs.append(jnp.zeros((STATE_DIM, WIN), BF16))
        write(b, dot(jnp.concatenate(lhs, axis=1), jnp.concatenate(rhs, axis=0)))
        if b < N_SPACE - 1:
            kept = jnp.exp(totals[b] - cum)
            kept = [(b_turned * kept[h : h + 1]).astype(BF16) for h in range(3)]
            local = dot(jnp.concatenate(kept, axis=0), window.astype(BF16))
            local = [local[STATE_DIM * h : STATE_DIM * (h + 1)] for h in range(3)]
            if carry is not None:
                fade = jnp.exp(totals[b])
                fade = jnp.concatenate([fade, fade], axis=1)
                local = [a + fade[h : h + 1] * c for h, (a, c) in enumerate(zip(local, carry))]
            carry = local


def scan_finish(
    ids, in_ref, y_ref, z_ref, row_ref, col_ref, before_ref, swapped_ref, core_ref, gain_ref, out_ref
):
    odd = ids[2] % 2
    same = ones_where(iota((WIN, WIN), 0) // 64 == iota((WIN, WIN), 1) // 64)
    group = iota((STATE_DIM, WIN), 1) // 64
    core = ids[0] % 2
    states = []
    for n in range(2):
        state = jnp.where(core == n, before_ref[...].astype(F32), swapped_ref[...].astype(F32))
        first = from_sent(core_ref[n])
        decay = jnp.exp(first[STATE_DIM : STATE_DIM + 1])
        state = jnp.where(core == 1, decay * state + first[:STATE_DIM], state)
        states += [jnp.where(group == h + odd, state, 0.0).astype(BF16) for h in range(3)]
    states = jnp.concatenate(states, axis=0)
    gain = gain_ref[...]
    for s in range(N_SPACE):
        here = slice(s * TOKENS, (s + 1) * TOKENS)
        c_turned = in_ref[s, :, WIN:].astype(F32).T[STATE_DIM:]
        scaled = []
        for ref in (row_ref, col_ref):
            decay = jnp.exp(ref[s])
            scaled += [c_turned * decay[h : h + 1] for h in range(3)]
        scaled = [
            jnp.concatenate(scaled[2 * n : 2 * n + 2], axis=0).T.astype(BF16) for n in range(3)
        ]
        total = jnp.concatenate([y_ref[t, here, :] + z_ref[t, here, :] for t in range(2)], axis=1)
        total = total + dot(jnp.concatenate(scaled, axis=1), states)
        meansq = dot((total * total).astype(BF16), same) * (1.0 / SCAN_DIM)
        normed = total * lax.rsqrt(meansq + EPS) * gain
        left, right = normed[:, :128], normed[:, 128:]
        full = jnp.where(odd == 1, right, left)
        part = jnp.where(odd == 1, left, right)
        out_ref[s, :TOKENS, :] = full.astype(BF16)
        out_ref[s, TOKENS:, :] = (part[:64] + pltpu.roll(part[64:], 64, 1)).astype(BF16)


SENT = STATE_DIM + 16


def to_send(state):
    high, low = split_high(state[STATE_DIM:])
    return jnp.concatenate([state[:STATE_DIM].astype(BF16), high, low], axis=0)


def from_sent(sent):
    sent = sent.astype(F32)
    decay = sent[STATE_DIM : STATE_DIM + 8] + sent[STATE_DIM + 8 :]
    return jnp.concatenate([sent[:STATE_DIM], decay], axis=0)


def join(earlier, later):
    decay = jnp.exp(later[STATE_DIM : STATE_DIM + 1])
    return jnp.where(iota((ROWS, WIN), 0) < STATE_DIM, decay, 1.0) * earlier + later


def chip_state(ids, own_ref, got_ref, total_ref, sent_ref):
    core = ids[0] % 2
    at = pl.ds(pl.multiple_of(core * ROWS, 8), ROWS)
    own, other = own_ref[at, :], from_sent(got_ref[core])
    first = core == 0
    total = join(jnp.where(first, own, other), jnp.where(first, other, own))
    total_ref[...] = total
    sent_ref[...] = to_send(total)


def grow(bit, ids, got_ref, total_in, *rest):
    before_in, (before_ref, total_ref, sent_ref) = (rest[0], rest[1:]) if bit > 2 else (None, rest)
    other, total = from_sent(got_ref[...]), total_in[...]
    later = (ids[3] & bit) > 0
    before = other if before_in is None else join(other, before_in[...])
    before_ref[...] = jnp.where(later, before, 0.0 if before_in is None else before_in[...])
    total = join(jnp.where(later, other, total), jnp.where(later, total, other))
    total_ref[...] = total
    sent_ref[...] = to_send(total)


def last_before(ids, got_ref, before_in, sent_ref):
    before = before_in[...]
    before = jnp.where((ids[3] & 16) > 0, join(from_sent(got_ref[...]), before), before)
    sent_ref[...] = before[:STATE_DIM].astype(BF16)


def add_up(ids, scan_ref, *rest):
    group = ids[0]
    out_ref, total = rest[4], rest[5]
    low_half = iota((64, 128), 1) < 64
    for k in range(4):
        even, uneven = scan_ref[2 * k], scan_ref[2 * k + 1]
        e, o = even[TOKENS:].astype(F32), uneven[TOKENS:].astype(F32)
        total[:, 384 * k : 384 * k + 128] = even[:TOKENS].astype(F32)
        total[:64, 384 * k + 128 : 384 * k + 256] = jnp.where(low_half, e, o)
        total[64:, 384 * k + 128 : 384 * k + 256] = jnp.where(
            low_half, pltpu.roll(e, 64, 1), pltpu.roll(o, 64, 1)
        )
        total[:, 384 * k + 256 : 384 * k + 384] = uneven[:TOKENS].astype(F32)
    for i in range(4):
        cols = pl.ds(pl.multiple_of((group ^ i) * GROUP, 128), GROUP)
        out_ref[:, cols] = (total[:, cols] + rest[i][...].astype(F32)).astype(BF16)


def tie(*values):
    return lax.optimization_barrier(values)


def z_shift(array, by):
    pairs = []
    for half in range(2):
        for z in range(8):
            for core in range(2):
                pairs.append((16 * half + 2 * z + core, 16 * half + 2 * ((z + by) % 8) + core))
    return lax.ppermute(array, "tm", pairs)


def partner(array, bits):
    return lax.ppermute(array, "tm", [(i, i ^ bits) for i in range(N_TM)])


def on_device(queries, keys, values, tile_mask, inner_x, bc_proj, log_decay, col_order, norm_gain):
    frame = lax.axis_index("tm")
    tile = lax.axis_index("space")
    group = 2 * (frame // 16) + frame % 2
    ids = jnp.stack([group, (frame // 2) % 8, tile, frame]).astype(jnp.int32)

    qkv = jax.ShapeDtypeStruct((3, TOKENS, GROUP), BF16)
    own, to_core, to_half, to_both = call(
        head_groups, (qkv,) * 4, 1, 3, 1, vmem=56
    )(ids, queries, keys, values)
    from_core = partner(to_core, 1)
    from_half = partner(to_half, 16)
    from_both = partner(to_both, 17)
    inner_x, _ = tie(inner_x, from_core)
    sent = call(
        scan_pack, jax.ShapeDtypeStruct((N_SPACE, TOKENS, WIN + 128), BF16), 0, 3, 1.5, vmem=56
    )(inner_x, bc_proj, log_decay)
    frame_in = lax.all_to_all(sent, "space", split_axis=0, concat_axis=0, tiled=True)
    (own, from_core), _ = tie((own, from_core), sent)
    chunks = {(0, 0): jnp.stack([own[1:], from_core[1:]])}

    def pass_on(source, step, after=None):
        if after is not None:
            behind, _ = tie(pair(source, step - 1), after)
            chunks[source, step - 1], chunks[source, 1 - step] = behind
        for sign in (1, -1):
            chunks[source, sign * step] = z_shift(chunks[source, sign * (step - 1)], -sign)

    def pair(source, step):
        return chunks[source, step], chunks[source, -step]

    def step_of(step, flash):
        return call(functools.partial(attend_step, step), STATE, 2, 8, 2.5)(
            ids, tile_mask, q_all, *pair(0, step), *pair(1, step), *flash
        )

    pass_on(0, 1)
    pass_on(0, 2)
    chunks[1, 0] = jnp.stack([from_half[1:], from_both[1:]])
    pass_on(1, 1)
    cum = jax.ShapeDtypeStruct((N_SPACE, 8, TOKENS), F32)
    one, sent = jax.ShapeDtypeStruct((ROWS, WIN), F32), jax.ShapeDtypeStruct((SENT, WIN), BF16)
    row_cum, col_cum, state, both_sent = call(
        scan_state,
        (
            cum,
            cum,
            jax.ShapeDtypeStruct((2 * ROWS, WIN), F32),
            jax.ShapeDtypeStruct((2, SENT, WIN), BF16),
        ),
        2,
        1,
        2,
    )(ids, col_order, frame_in)
    core_sent = partner(both_sent, 1)
    total, walk = call(chip_state, (one, sent), 1, 2, 0.5)(ids, state, core_sent)

    other = partner(walk, 2)
    frame_tokens = N_SPACE * TOKENS
    wide = jax.ShapeDtypeStruct((2, frame_tokens, 128), F32)
    inside_in, _ = tie(frame_in, walk)
    y_row = call(
        functools.partial(scan_inside, False), wide, 2, 1, 2, [pltpu.VMEM((8, 128), F32)]
    )(ids, col_order, inside_in)
    pass_on(0, 3, y_row)
    other, y_row = tie(other, y_row)
    before, total, walk = call(functools.partial(grow, 2), (one, one, sent), 1, 2, 0.5)(
        ids, other, total
    )

    other = partner(walk, 4)
    own, _ = tie(own, walk)
    *flash, q_all = call(
        attend_own, STATE + (jax.ShapeDtypeStruct((2, 2, TOKENS, GROUP), BF16),), 2, 4, 2
    )(ids, tile_mask, own, from_core, from_half, from_both)
    pass_on(1, 2, flash)
    flash = step_of(1, flash)
    other, flash = tie(other, flash)
    before, total, walk = call(functools.partial(grow, 4), (one, one, sent), 1, 3, 0.5)(
        ids, other, total, before
    )

    other = partner(walk, 14)
    inside_in, _ = tie(frame_in, walk)
    y_col = call(
        functools.partial(scan_inside, True),
        wide,
        2,
        1,
        4,
        [pltpu.VMEM((2, 3, frame_tokens, 128), F32)],
    )(ids, col_order, inside_in)
    other, y_col = tie(other, y_col)
    before, total, walk = call(functools.partial(grow, 8), (one, one, sent), 1, 3, 0.5)(
        ids, other, total, before
    )

    other = partner(walk, 16)
    pass_on(1, 3, walk)
    flash, _ = tie(flash, walk)
    flash = step_of(2, flash)
    other, flash = tie(other, flash)
    before = call(last_before, jax.ShapeDtypeStruct((STATE_DIM, WIN), BF16), 1, 2, 0.5)(
        ids, other, before
    )
    before_other = partner(before, 1)
    (to_up, to_down), _ = tie((chunks[0, 3], chunks[1, -3]), before)
    far_a, far_b = z_shift(to_up, -1), z_shift(to_down, 1)

    gain = lax.dynamic_slice(norm_gain, (384 * (tile // 2) + 128 * (tile % 2),), (WIN,))
    normed = call(scan_finish, jax.ShapeDtypeStruct((N_SPACE, 192, 128), BF16), 1, 9, 3)(
        ids,
        frame_in,
        y_row,
        y_col,
        row_cum,
        col_cum,
        before,
        before_other,
        core_sent,
        gain.reshape(1, WIN),
    )
    scan_rows = lax.all_to_all(normed, "space", split_axis=0, concat_axis=0, tiled=True)
    flash, _ = tie(flash, normed)
    flash = step_of(3, flash)
    piece = jax.ShapeDtypeStruct((TOKENS, GROUP), BF16)
    pieces = {}
    for u in (1, 0):
        pieces[u] = call(functools.partial(attend_last, u), (piece, piece), 2, 6, 2)(
            ids, tile_mask, q_all, far_a, far_b, *flash
        )
        flash, pieces[u] = tie(flash, pieces[u])
    attention = (
        pieces[0][0],
        partner(pieces[0][1], 1),
        partner(pieces[1][0], 16),
        partner(pieces[1][1], 17),
    )
    return call(
        add_up,
        jax.ShapeDtypeStruct((TOKENS, HEADS * HEAD_DIM), BF16),
        1,
        5,
        1.5,
        [pltpu.VMEM((TOKENS, HEADS * HEAD_DIM), F32)],
    )(ids, scan_rows, *attention)


def solution(mesh):
    return jax.shard_map(
        on_device,
        mesh=mesh,
        in_specs=(
            P(("tm", "space"), None),
            P(("tm", "space"), None),
            P(("tm", "space"), None),
            P(),
            P(("tm", "space"), None),
            P(("tm", "space"), None),
            P(None, ("tm", "space")),
            P(),
            P(),
        ),
        out_specs=P(("tm", "space"), None),
        check_vma=False,
    )
```

```python
import functools
import math

import jax
import jax.numpy as jnp
from jax import lax
from jax.experimental import pallas as pl
from jax.experimental.pallas import tpu as pltpu
from jax.sharding import PartitionSpec as P

HEADS = 12
HEAD_DIM = 128
SCAN_HEADS = 24
SCAN_DIM = 64
STATE_DIM = 64
COLS = 32
TOKENS = 128
N_TM = 32
N_SPACE = 8
GROUP = HEADS // 4 * HEAD_DIM
WIN = 256
ROWS = STATE_DIM + 8

COST = 0.001
EPS = 1e-05
FLOOR = -1e30
LOG2_SCALE = HEAD_DIM ** (-0.5) * math.log2(math.e)
BF16 = jnp.bfloat16
F32 = jnp.float32

VMEM = pl.BlockSpec(memory_space=pltpu.VMEM)
SMEM = pl.BlockSpec(memory_space=pltpu.SMEM)


def call(body, out_shape, n_smem, n_vmem, us, scratch=(), vmem=16):
    return pl.pallas_call(
        body,
        out_shape=out_shape,
        in_specs=[SMEM] * n_smem + [VMEM] * n_vmem,
        out_specs=jax.tree.map(lambda _: VMEM, out_shape),
        scratch_shapes=list(scratch),
        name=getattr(body, "func", body).__name__,
        compiler_params=pltpu.CompilerParams(vmem_limit_bytes=vmem * 2**20),
        cost_estimate=pl.CostEstimate(
            flops=int(us * 1.1e9 * COST), bytes_accessed=int(us * 3e6 * COST), transcendentals=0
        ),
    )


def dot(a, b, contract=(1, 0)):
    return lax.dot_general(
        a, b, (((contract[0],), (contract[1],)), ((), ())), preferred_element_type=F32
    )


def iota(shape, axis):
    return lax.broadcasted_iota(jnp.int32, shape, axis)


def head_groups(ids, q_ref, k_ref, v_ref, *outs):
    for i, out in enumerate(outs):
        cols = pl.ds(pl.multiple_of((ids[0] ^ i) * GROUP, 128), GROUP)
        for t, ref in enumerate((q_ref, k_ref, v_ref)):
            out[t] = ref[:, cols]


STATE = (
    jax.ShapeDtypeStruct((2, 8, 2 * TOKENS), F32),
    jax.ShapeDtypeStruct((2, 8, 2 * TOKENS), F32),
    jax.ShapeDtypeStruct((2, HEADS // 4, HEAD_DIM, 2 * TOKENS), F32),
)


def absorb(ids, mask_ref, q_ref, u, sources, state):
    group, place = ids[0], ids[1]
    half, core = group // 2, group % 2
    lanes = iota((1, 2 * TOKENS), 1)
    biases = []
    for _, half_k, place_k in sources:
        for j in range(2):
            frame_k = 16 * half_k + 2 * place_k + (core ^ j)
            seen = [
                jnp.where(mask_ref[16 * (half ^ u) + 2 * place + (core ^ a), frame_k] > 0, 0.0, FLOOR)
                for a in range(2)
            ]
            biases.append(jnp.where(lanes < TOKENS, seen[0], seen[1]).astype(F32))
    new = []
    for h in range(GROUP // HEAD_DIM):
        cols = slice(h * HEAD_DIM, (h + 1) * HEAD_DIM)
        q = q_ref[u, :, :, cols].reshape(2 * TOKENS, HEAD_DIM)
        k = jnp.concatenate([load(0, cols) for load, _, _ in sources], axis=0)
        v = jnp.concatenate([load(1, cols) for load, _, _ in sources], axis=0)
        scores = dot(k, q, (1, 1))
        parts = [scores[i * TOKENS : (i + 1) * TOKENS] for i in range(len(biases))]
        tops = [
            jnp.max(s, axis=0, keepdims=True) * LOG2_SCALE + bias for s, bias in zip(parts, biases)
        ]
        top = functools.reduce(jnp.maximum, tops)
        if state is not None:
            old, total_in, acc_in = state[h]
            top = jnp.maximum(top, old)
        probs = [jnp.exp2(s * LOG2_SCALE + (bias - top)) for s, bias in zip(parts, biases)]
        pb = jnp.concatenate([p.astype(BF16) for p in probs], axis=0); total = dot(jnp.ones((8, pb.shape[0]), BF16), pb)[:1]
        update = dot(v, pb, (0, 0))
        if state is not None:
            factor = jnp.exp2(old - top)
            total = total_in * factor + total
            update = acc_in * factor + update
        new.append((top, total, update))
    return new


def loader(ref):
    return lambda t, cols: ref[:, t, :, cols].reshape(2 * TOKENS, HEAD_DIM)


def either(first, a_ref, b_ref):
    a, b = loader(a_ref), loader(b_ref)
    return lambda t, cols: jnp.where(first, a(t, cols), b(t, cols))


def read_state(u, m_ref, l_ref, acc_ref):
    return [
        (m_ref[u, h : h + 1, :], l_ref[u, h : h + 1, :], acc_ref[u, h])
        for h in range(GROUP // HEAD_DIM)
    ]


def write_state(u, new, m_ref, l_ref, acc_ref):
    for h, (top, total, acc) in enumerate(new):
        m_ref[u, h : h + 1, :] = top
        l_ref[u, h : h + 1, :] = total
        acc_ref[u, h] = acc
    rest = jnp.zeros((8 - len(new), 2 * TOKENS), F32)
    m_ref[u, len(new) :, :] = rest
    l_ref[u, len(new) :, :] = rest


def attend_own(ids, mask_ref, own, core, other, both, m_ref, l_ref, acc_ref, q_out):
    half = ids[0] // 2
    for u, pair in enumerate(((own, core), (other, both))):
        q_out[u, 0], q_out[u, 1] = pair[0][0], pair[1][0]
    for u, (first, second) in enumerate(((own, core), (other, both))):

        def load(t, cols):
            return jnp.concatenate([first[t + 1, :, cols], second[t + 1, :, cols]], axis=0)

        new = absorb(ids, mask_ref, q_out, u, [(load, half ^ u, ids[1])], None)
        write_state(u, new, m_ref, l_ref, acc_ref)


def attend_step(step, ids, mask_ref, q_ref, a_up, a_down, b_up, b_down, *states):
    half, place = ids[0] // 2, ids[1]
    above, below = place + step, place - step
    for u in range(2):
        flip_up, flip_down = u ^ (above // 8), u ^ jnp.where(below < 0, 1, 0)
        sources = [
            (either(flip_up == 0, a_up, b_up), half ^ flip_up, above % 8),
            (either(flip_down == 0, a_down, b_down), half ^ flip_down, (below + 8) % 8),
        ]
        new = absorb(ids, mask_ref, q_ref, u, sources, read_state(u, *states[:3]))
        write_state(u, new, *states[3:])


def attend_last(u, ids, mask_ref, q_ref, a_ref, b_ref, m_in, l_in, acc_in, *outs):
    half, far = ids[0] // 2, (ids[1] + 4) % 8
    sources = [(loader(a_ref), half, far), (loader(b_ref), half ^ 1, far)]
    state = read_state(u, m_in, l_in, acc_in)
    for h, (_, total, acc) in enumerate(absorb(ids, mask_ref, q_ref, u, sources, state)):
        out = (acc / total).T.astype(BF16)
        cols = slice(h * HEAD_DIM, (h + 1) * HEAD_DIM)
        outs[0][:, cols] = out[:TOKENS]
        outs[1][:, cols] = out[TOKENS:]


def scan_pack(x_ref, bc_ref, log_ref, out_ref):
    lanes = iota((TOKENS, 128), 1)
    logs = log_ref[...].astype(F32)
    turned = pltpu.roll(logs, 64, 1)
    bc = bc_ref[...]
    for s in range(N_SPACE):
        base = 384 * (s // 2) + 128 * (s % 2)
        out_ref[s, :, :WIN] = x_ref[:, base : base + WIN]
        out_ref[s, :, WIN:] = bc
        heads, spun = logs[3 * s : 3 * s + 3], turned[3 * s : 3 * s + 3]
        rows = [heads, spun] if s % 2 else [spun, heads]
        rows = jnp.concatenate(rows + [jnp.zeros((10, 128), F32)], axis=0)
        at = slice(0, 128) if s % 2 else slice(128, 256)
        free = lanes[:16] < 64 if s % 2 else lanes[:16] >= 64
        out_ref[s, :16, at] = jnp.where(free, rows, out_ref[s, :16, at].astype(F32)).astype(BF16)


def split_high(a):
    high = a.astype(BF16)
    return high, (a - high.astype(F32)).astype(BF16)


def ones_where(condition):
    return jnp.where(condition, 1.0, 0.0).astype(BF16)


def log_rows(in_ref, odd):
    low = iota((8, 128), 1) < 64
    keep = iota((8, 128), 0) < 3
    tiles = []
    for s in range(N_SPACE):
        left, right = in_ref[s, :16, :128].astype(F32)[:8], in_ref[s, :16, 128:WIN].astype(F32)[:8]
        first = jnp.where(odd == 1, left, pltpu.roll(right, 64, 1))
        second = pltpu.roll(first, 64, 1)
        second = jnp.concatenate([second[3:], second[:3]], axis=0)
        tiles.append(jnp.where(keep, jnp.where(low, first, second), 0.0))
    return jnp.concatenate(tiles, axis=0).astype(BF16)


def stacked(rows, weights):
    out = dot(rows, weights)
    return [out[8 * s : 8 * s + 8] for s in range(N_SPACE)]


def running(parts):
    sums = [jnp.zeros_like(parts[0])]
    for part in parts:
        sums.append(sums[-1] + part)
    return sums[:-1], sums[-1]


def heads_diagonal(blocks, group, odd):
    return functools.reduce(
        jnp.add, [jnp.where(group == h + odd, block, 0.0) for h, block in enumerate(blocks)]
    )


def scan_state(ids, order_ref, in_ref, row_ref, col_ref, state_ref, sent_ref):
    odd = ids[2] % 2
    logs = log_rows(in_ref, odd)
    i, j = iota((TOKENS, TOKENS), 0), iota((TOKENS, TOKENS), 1)
    every = jnp.ones((TOKENS, TOKENS), BF16)
    row_before, total = running(stacked(logs, every))
    row_cum = [a + b for a, b in zip(stacked(logs, ones_where(i <= j)), row_before)]

    rank = jnp.zeros((TOKENS, TOKENS), F32)
    for k in range(COLS):
        rank = jnp.where(j % COLS == order_ref[k], float(k), rank)
    same_col = i % COLS == j % COLS
    earlier = stacked(logs, ones_where(rank.T < rank))
    earlier = functools.reduce(jnp.add, earlier)
    col_before, _ = running(stacked(logs, ones_where(same_col)))
    within = stacked(logs, ones_where(same_col & (i <= j)))
    col_cum = [a + b + earlier for a, b in zip(within, col_before)]

    group = iota((STATE_DIM, WIN), 1) // 64
    state = [jnp.zeros((STATE_DIM, WIN), F32)] * 6
    for s in range(N_SPACE):
        row_ref[s], col_ref[s] = row_cum[s], col_cum[s]
        b_turned = in_ref[s, :, WIN:].astype(F32).T[:STATE_DIM]
        lhs = []
        for cum in (row_cum[s], col_cum[s]):
            kept = jnp.exp(total - cum)
            lhs += [(b_turned * kept[h : h + 1]).astype(BF16) for h in range(3)]
        out = dot(jnp.concatenate(lhs, axis=0), in_ref[s, :, :WIN])
        state = [a + out[STATE_DIM * n : STATE_DIM * (n + 1)] for n, a in enumerate(state)]
    wide = jnp.concatenate([total, total], axis=1)
    lane_total = heads_diagonal(
        [jnp.broadcast_to(wide[h : h + 1], (8, WIN)) for h in range(3)], group[:8], odd
    )
    for n in range(2):
        at = n * ROWS
        own = heads_diagonal(state[3 * n : 3 * n + 3], group, odd)
        own = jnp.concatenate([own, lane_total], axis=0)
        state_ref[at : at + ROWS, :] = own
        sent_ref[n] = to_send(own)


def scan_inside(by_column, ids, order_ref, in_ref, *rest):
    odd = ids[2] % 2
    y_ref, buf = rest

    def strided(s, t):
        return in_ref[s, :, t * 128 : (t + 1) * 128].astype(F32)

    if by_column:
        rows, buf = buf.at[0], buf.at[1]
        for s in range(N_SPACE):
            for t in range(3):
                rows[t, s * TOKENS : (s + 1) * TOKENS, :] = strided(s, t)
        for k in range(COLS):
            for t in range(3):
                buf[t, k * 32 : (k + 1) * 32, :] = rows[t, pl.ds(order_ref[k], 32, stride=COLS), :]

    def load(b, t):
        return buf[t, b * TOKENS : (b + 1) * TOKENS, :] if by_column else strided(b, t)

    i, j = iota((TOKENS, TOKENS), 0), iota((TOKENS, TOKENS), 1)
    lower_mask = i >= j
    upper = ones_where(i <= j)
    every = jnp.ones((TOKENS, TOKENS), BF16)
    logs = log_rows(in_ref, odd)
    tile_of = (iota((8, TOKENS), 1) % 32) // 4
    col_logs = []
    for b in range(N_SPACE) if by_column else ():
        column = jnp.zeros((TOKENS, TOKENS), jnp.int32)
        for k in range(4):
            column = jnp.where(j // 32 == k, order_ref[4 * b + k], column)
        picked = stacked(logs, ones_where((i % COLS == column) & (i // COLS == j % 4)))
        log = jnp.zeros((8, TOKENS), F32)
        for s in range(N_SPACE):
            log = jnp.where(tile_of == s, picked[s], log)
        col_logs.append(log)
    if by_column:
        logs = jnp.concatenate(col_logs, axis=0).astype(BF16)

    group = iota((TOKENS, WIN), 1) // 64
    state_group = iota((STATE_DIM, WIN), 1) // 64

    def write_row(b, out):
        for t in range(2):
            y_ref[t, b * TOKENS : (b + 1) * TOKENS, :] = out[:, t * 128 : (t + 1) * 128]

    def write_col(b, out):
        for k in range(TOKENS // 32):
            here = pl.ds(order_ref[b * 4 + k], 32, stride=COLS)
            for t in range(2):
                part = out[k * 32 : (k + 1) * 32, t * 128 : (t + 1) * 128]
                y_ref[t, here, :] = part

    write = write_col if by_column else write_row
    carry = None
    cums, totals = stacked(logs, upper), stacked(logs, every)
    for b in range(N_SPACE):
        window = jnp.concatenate([load(b, 0), load(b, 1)], axis=1)
        bc = load(b, 2)
        turned, bc = bc.T, bc.astype(BF16)
        b_turned, c_turned = turned[:STATE_DIM], turned[STATE_DIM:]
        scores = dot(bc[:, STATE_DIM:], bc[:, :STATE_DIM], (1, 1))
        cum = cums[b]
        lhs, rhs = [], []
        for h in range(3):
            cum_j = jnp.broadcast_to(cum[h : h + 1], (TOKENS, TOKENS))
            gap = jnp.where(lower_mask, cum_j.T - cum_j, FLOOR)
            lhs.append((scores * jnp.exp(gap)).astype(BF16))
            rhs.append(jnp.where(group == h + odd, window, 0.0).astype(BF16))
        if carry is not None:
            decay = jnp.exp(cum)
            scaled = [c_turned * decay[h : h + 1] for h in range(3)]
            scaled.append(jnp.zeros_like(c_turned))
            scaled = jnp.concatenate(scaled, axis=0)
            lhs += [scaled[:128].T.astype(BF16), scaled[128:].T.astype(BF16)]
            for h in range(3):
                rhs.append(jnp.where(state_group == h + odd, carry[h], 0.0).astype(BF16))
            rhs.append(jnp.zeros((STATE_DIM, WIN), BF16))
        write(b, dot(jnp.concatenate(lhs, axis=1), jnp.concatenate(rhs, axis=0)))
        if b < N_SPACE - 1:
            kept = jnp.exp(totals[b] - cum)
            kept = [(b_turned * kept[h : h + 1]).astype(BF16) for h in range(3)]
            local = dot(jnp.concatenate(kept, axis=0), window.astype(BF16))
            local = [local[STATE_DIM * h : STATE_DIM * (h + 1)] for h in range(3)]
            if carry is not None:
                fade = jnp.exp(totals[b])
                fade = jnp.concatenate([fade, fade], axis=1)
                local = [a + fade[h : h + 1] * c for h, (a, c) in enumerate(zip(local, carry))]
            carry = local


def scan_finish(
    ids, in_ref, y_ref, z_ref, row_ref, col_ref, before_ref, swapped_ref, core_ref, gain_ref, out_ref
):
    odd = ids[2] % 2
    same = ones_where(iota((WIN, WIN), 0) // 64 == iota((WIN, WIN), 1) // 64)
    group = iota((STATE_DIM, WIN), 1) // 64
    core = ids[0] % 2
    states = []
    for n in range(2):
        state = jnp.where(core == n, before_ref[...].astype(F32), swapped_ref[...].astype(F32))
        first = from_sent(core_ref[n])
        decay = jnp.exp(first[STATE_DIM : STATE_DIM + 1])
        state = jnp.where(core == 1, decay * state + first[:STATE_DIM], state)
        states += [jnp.where(group == h + odd, state, 0.0).astype(BF16) for h in range(3)]
    states = jnp.concatenate(states, axis=0)
    gain = gain_ref[...]
    for s in range(N_SPACE):
        here = slice(s * TOKENS, (s + 1) * TOKENS)
        c_turned = in_ref[s, :, WIN:].astype(F32).T[STATE_DIM:]
        scaled = []
        for ref in (row_ref, col_ref):
            decay = jnp.exp(ref[s])
            scaled += [c_turned * decay[h : h + 1] for h in range(3)]
        scaled = [
            jnp.concatenate(scaled[2 * n : 2 * n + 2], axis=0).T.astype(BF16) for n in range(3)
        ]
        total = jnp.concatenate([y_ref[t, here, :] + z_ref[t, here, :] for t in range(2)], axis=1)
        total = total + dot(jnp.concatenate(scaled, axis=1), states)
        meansq = dot((total * total).astype(BF16), same) * (1.0 / SCAN_DIM)
        normed = total * lax.rsqrt(meansq + EPS) * gain
        left, right = normed[:, :128], normed[:, 128:]
        full = jnp.where(odd == 1, right, left)
        part = jnp.where(odd == 1, left, right)
        out_ref[s, :TOKENS, :] = full.astype(BF16)
        out_ref[s, TOKENS:, :] = (part[:64] + pltpu.roll(part[64:], 64, 1)).astype(BF16)


SENT = STATE_DIM + 16


def to_send(state):
    high, low = split_high(state[STATE_DIM:])
    return jnp.concatenate([state[:STATE_DIM].astype(BF16), high, low], axis=0)


def from_sent(sent):
    sent = sent.astype(F32)
    decay = sent[STATE_DIM : STATE_DIM + 8] + sent[STATE_DIM + 8 :]
    return jnp.concatenate([sent[:STATE_DIM], decay], axis=0)


def join(earlier, later):
    decay = jnp.exp(later[STATE_DIM : STATE_DIM + 1])
    return jnp.where(iota((ROWS, WIN), 0) < STATE_DIM, decay, 1.0) * earlier + later


def chip_state(ids, own_ref, got_ref, total_ref, sent_ref):
    core = ids[0] % 2
    at = pl.ds(pl.multiple_of(core * ROWS, 8), ROWS)
    own, other = own_ref[at, :], from_sent(got_ref[core])
    first = core == 0
    total = join(jnp.where(first, own, other), jnp.where(first, other, own))
    total_ref[...] = total
    sent_ref[...] = to_send(total)


def grow(bit, ids, got_ref, total_in, *rest):
    before_in, (before_ref, total_ref, sent_ref) = (rest[0], rest[1:]) if bit > 2 else (None, rest)
    other, total = from_sent(got_ref[...]), total_in[...]
    later = (ids[3] & bit) > 0
    before = other if before_in is None else join(other, before_in[...])
    before_ref[...] = jnp.where(later, before, 0.0 if before_in is None else before_in[...])
    total = join(jnp.where(later, other, total), jnp.where(later, total, other))
    total_ref[...] = total
    sent_ref[...] = to_send(total)


def last_before(ids, got_ref, before_in, sent_ref):
    before = before_in[...]
    before = jnp.where((ids[3] & 16) > 0, join(from_sent(got_ref[...]), before), before)
    sent_ref[...] = before[:STATE_DIM].astype(BF16)


def add_up(ids, scan_ref, *rest):
    group = ids[0]
    out_ref, total = rest[4], rest[5]
    low_half = iota((64, 128), 1) < 64
    for k in range(4):
        even, uneven = scan_ref[2 * k], scan_ref[2 * k + 1]
        e, o = even[TOKENS:].astype(F32), uneven[TOKENS:].astype(F32)
        total[:, 384 * k : 384 * k + 128] = even[:TOKENS].astype(F32)
        total[:64, 384 * k + 128 : 384 * k + 256] = jnp.where(low_half, e, o)
        total[64:, 384 * k + 128 : 384 * k + 256] = jnp.where(
            low_half, pltpu.roll(e, 64, 1), pltpu.roll(o, 64, 1)
        )
        total[:, 384 * k + 256 : 384 * k + 384] = uneven[:TOKENS].astype(F32)
    for i in range(4):
        cols = pl.ds(pl.multiple_of((group ^ i) * GROUP, 128), GROUP)
        out_ref[:, cols] = (total[:, cols] + rest[i][...].astype(F32)).astype(BF16)


def tie(*values):
    return lax.optimization_barrier(values)


def z_shift(array, by):
    pairs = []
    for half in range(2):
        for z in range(8):
            for core in range(2):
                pairs.append((16 * half + 2 * z + core, 16 * half + 2 * ((z + by) % 8) + core))
    return lax.ppermute(array, "tm", pairs)


def partner(array, bits):
    return lax.ppermute(array, "tm", [(i, i ^ bits) for i in range(N_TM)])


def on_device(queries, keys, values, tile_mask, inner_x, bc_proj, log_decay, col_order, norm_gain):
    frame = lax.axis_index("tm")
    tile = lax.axis_index("space")
    group = 2 * (frame // 16) + frame % 2
    ids = jnp.stack([group, (frame // 2) % 8, tile, frame]).astype(jnp.int32)

    qkv = jax.ShapeDtypeStruct((3, TOKENS, GROUP), BF16)
    own, to_core, to_half, to_both = call(
        head_groups, (qkv,) * 4, 1, 3, 1, vmem=56
    )(ids, queries, keys, values)
    from_core = partner(to_core, 1)
    from_half = partner(to_half, 16)
    from_both = partner(to_both, 17)
    inner_x, _ = tie(inner_x, from_core)
    sent = call(
        scan_pack, jax.ShapeDtypeStruct((N_SPACE, TOKENS, WIN + 128), BF16), 0, 3, 1.5, vmem=56
    )(inner_x, bc_proj, log_decay)
    frame_in = lax.all_to_all(sent, "space", split_axis=0, concat_axis=0, tiled=True)
    (own, from_core), _ = tie((own, from_core), sent)
    chunks = {(0, 0): jnp.stack([own[1:], from_core[1:]])}

    def pass_on(source, step, after=None):
        if after is not None:
            behind, _ = tie(pair(source, step - 1), after)
            chunks[source, step - 1], chunks[source, 1 - step] = behind
        for sign in (1, -1):
            chunks[source, sign * step] = z_shift(chunks[source, sign * (step - 1)], -sign)

    def pair(source, step):
        return chunks[source, step], chunks[source, -step]

    def step_of(step, flash):
        return call(functools.partial(attend_step, step), STATE, 2, 8, 2.5)(
            ids, tile_mask, q_all, *pair(0, step), *pair(1, step), *flash
        )

    pass_on(0, 1)
    pass_on(0, 2)
    chunks[1, 0] = jnp.stack([from_half[1:], from_both[1:]])
    pass_on(1, 1)
    cum = jax.ShapeDtypeStruct((N_SPACE, 8, TOKENS), F32)
    one, sent = jax.ShapeDtypeStruct((ROWS, WIN), F32), jax.ShapeDtypeStruct((SENT, WIN), BF16)
    row_cum, col_cum, state, both_sent = call(
        scan_state,
        (
            cum,
            cum,
            jax.ShapeDtypeStruct((2 * ROWS, WIN), F32),
            jax.ShapeDtypeStruct((2, SENT, WIN), BF16),
        ),
        2,
        1,
        2,
    )(ids, col_order, frame_in)
    core_sent = partner(both_sent, 1)
    total, walk = call(chip_state, (one, sent), 1, 2, 0.5)(ids, state, core_sent)

    other = partner(walk, 2)
    frame_tokens = N_SPACE * TOKENS
    wide = jax.ShapeDtypeStruct((2, frame_tokens, 128), F32)
    inside_in, _ = tie(frame_in, walk)
    y_row = call(
        functools.partial(scan_inside, False), wide, 2, 1, 2, [pltpu.VMEM((8, 128), F32)]
    )(ids, col_order, inside_in)
    pass_on(0, 3, y_row)
    other, y_row = tie(other, y_row)
    before, total, walk = call(functools.partial(grow, 2), (one, one, sent), 1, 2, 0.5)(
        ids, other, total
    )

    other = partner(walk, 4)
    own, _ = tie(own, walk)
    *flash, q_all = call(
        attend_own, STATE + (jax.ShapeDtypeStruct((2, 2, TOKENS, GROUP), BF16),), 2, 4, 2
    )(ids, tile_mask, own, from_core, from_half, from_both)
    pass_on(1, 2, flash)
    flash = step_of(1, flash)
    inside_in, _ = tie(frame_in, flash)
    y_col = call(
        functools.partial(scan_inside, True),
        wide,
        2,
        1,
        4,
        [pltpu.VMEM((2, 3, frame_tokens, 128), F32)],
    )(ids, col_order, inside_in)
    other, flash, y_col = tie(other, flash, y_col)
    before, total, walk = call(functools.partial(grow, 4), (one, one, sent), 1, 3, 0.5)(
        ids, other, total, before
    )

    other = partner(walk, 14)
    before, total, walk = call(functools.partial(grow, 8), (one, one, sent), 1, 3, 0.5)(
        ids, other, total, before
    )

    other = partner(walk, 16)
    pass_on(1, 3, walk)
    flash, _ = tie(flash, walk)
    flash = step_of(2, flash)
    other, flash = tie(other, flash)
    before = call(last_before, jax.ShapeDtypeStruct((STATE_DIM, WIN), BF16), 1, 2, 0.5)(
        ids, other, before
    )
    before_other = partner(before, 1)
    (to_up, to_down), _ = tie((chunks[0, 3], chunks[1, -3]), before)
    far_a, far_b = z_shift(to_up, -1), z_shift(to_down, 1)

    gain = lax.dynamic_slice(norm_gain, (384 * (tile // 2) + 128 * (tile % 2),), (WIN,))
    normed = call(scan_finish, jax.ShapeDtypeStruct((N_SPACE, 192, 128), BF16), 1, 9, 3)(
        ids,
        frame_in,
        y_row,
        y_col,
        row_cum,
        col_cum,
        before,
        before_other,
        core_sent,
        gain.reshape(1, WIN),
    )
    scan_rows = lax.all_to_all(normed, "space", split_axis=0, concat_axis=0, tiled=True)
    flash, _ = tie(flash, normed)
    flash = step_of(3, flash)
    piece = jax.ShapeDtypeStruct((TOKENS, GROUP), BF16)
    pieces = {}
    for u in (1, 0):
        pieces[u] = call(functools.partial(attend_last, u), (piece, piece), 2, 6, 2)(
            ids, tile_mask, q_all, far_a, far_b, *flash
        )
        flash, pieces[u] = tie(flash, pieces[u])
    attention = (
        pieces[0][0],
        partner(pieces[0][1], 1),
        partner(pieces[1][0], 16),
        partner(pieces[1][1], 17),
    )
    return call(
        add_up,
        jax.ShapeDtypeStruct((TOKENS, HEADS * HEAD_DIM), BF16),
        1,
        5,
        1.5,
        [pltpu.VMEM((TOKENS, HEADS * HEAD_DIM), F32)],
    )(ids, scan_rows, *attention)


def solution(mesh):
    return jax.shard_map(
        on_device,
        mesh=mesh,
        in_specs=(
            P(("tm", "space"), None),
            P(("tm", "space"), None),
            P(("tm", "space"), None),
            P(),
            P(("tm", "space"), None),
            P(("tm", "space"), None),
            P(None, ("tm", "space")),
            P(),
            P(),
        ),
        out_specs=P(("tm", "space"), None),
        check_vma=False,
    )
```
